512 devices in a mesh: grp: 8 (over x, core), sp: 64 (over z, y).
Axes of the slice: x: 4, y: 8, z: 8, core: 2. Of those that a mesh axis runs over, the one named last changes fastest.
Arguments:
- upper_out: bfloat16 [65536, 2048], P(('grp', 'sp')), may hold values from -6 to 6
- lower_out: bfloat16 [65536, 2048], P(('grp', 'sp')), may hold values from -6 to 6
- upper_grad: bfloat16 [65536, 2048], P(('grp', 'sp')), may hold values from -6 to 6
- lower_grad: bfloat16 [65536, 2048], P(('grp', 'sp')), may hold values from -6 to 6
- norm_gain: float32 [2048], replicated, may hold values from 0.5 to 1.5
- query_weight: bfloat16 [2048, 1024], P('sp')
- key_weight: bfloat16 [2048, 256], P('sp')
- value_matrix: bfloat16 [2048, 256], P('sp'), may hold values from -0.125 to 0.125
- out_weight: bfloat16 [1024, 2048], P('sp'), may hold values from -0.1875 to 0.1875
- route_table: int32 [8, 64, 8], P('grp', 'sp'), may hold values from 0 to 7, each once within a row
- doc_lengths: int32 [8, 32], P('grp'), may hold values from 1 to 512, 8192 in all within a row
Outputs:
- restored: bfloat16 [65536, 2048], P(('grp', 'sp'))
- back_grad: bfloat16 [65536, 2048], P(('grp', 'sp'))
The draws below stay inside these ranges and needn't reach their ends.
Inputs may be any that keep to these rules, and one draw needn't show every extreme that they name: `route_table`: each device's list of 8 destinations names every group once. `doc_lengths`: each group's 32 lengths sum to 8192; the longest is exactly 512.
All inputs are finite; a program needn't handle non-finite values.
Results may differ from the reference program's by a relative error of at most 0.015.
Values may be sent and summed in bfloat16 or wider, within the bound.
A program may use at most 64 MiB of HBM per device.

```python
import math
import jax
import jax.numpy as jnp
import numpy as np
from jax import lax

MODEL_WIDTH = 2048
QUERY_HEADS = 16
KEY_VALUE_HEADS = 4
HEAD_WIDTH = 64
TOK_DEV = 128
LONGEST = 512
GROUPS = 8
LANES = 64
GROUP_ROWS = 8192
TOKENS = 65536
DOCS = 32


def draw_query_weight(key, part):
    key = jax.random.fold_in(key, 11)
    random_jitter = jnp.clip(jax.random.normal(key, (MODEL_WIDTH, QUERY_HEADS * HEAD_WIDTH), jnp.float32), -6.0, 6.0)
    return (random_jitter / math.sqrt(MODEL_WIDTH)).astype(jnp.bfloat16)


def draw_key_weight(key, part):
    key = jax.random.fold_in(key, 12)
    random_jitter = jnp.clip(jax.random.normal(key, (MODEL_WIDTH, KEY_VALUE_HEADS * HEAD_WIDTH), jnp.float32), -6.0, 6.0)
    return (random_jitter / math.sqrt(MODEL_WIDTH)).astype(jnp.bfloat16)


def shard_levels(stream_key, extent, split, smallest, top_value):
    factor_of = 1.0
    for position, shards_of in split:
        heights = jax.random.uniform(jax.random.fold_in(jax.random.fold_in(stream_key, 6), position), (shards_of,), jnp.float32, smallest / len(split), top_value / len(split))
        factor_of = factor_of * jnp.repeat(jnp.exp(heights), extent[position] // shards_of).reshape((-1,) + (1,) * (len(extent) - 1 - position))
    return factor_of


def profile(amount, total, limit, lean):
    weights = [(1 << 20) // math.isqrt(rank ** lean) + 1 for rank in range(2, amount + 1)]
    surplus, given = total - limit - (amount - 1), [1] * (amount - 1)
    while surplus > 0:
        free = [i for i in range(amount - 1) if given[i] < limit]
        whole, budget = sum([weights[i] for i in free]), surplus
        for i in free:
            more = min(limit - given[i], max(1, budget * weights[i] // whole), surplus)
            given[i] = given[i] + more
            surplus = surplus - more
    return np.array([limit] + given)


def uneven_parts(key, amount, total, limit, slope):
    if amount == 2:
        one = jax.random.randint(key, (), max(1, total - limit), min(limit, total - 1) + 1)
        return jnp.stack([one, total - one])
    lengths = jnp.asarray(profile(amount, total, limit, slope), jnp.int32)
    twos = (amount - 1) // 2
    donor, taker = lengths[1:1 + 2 * twos:2], lengths[2:2 + 2 * twos:2]
    room = jnp.minimum(donor - 1, limit - taker)
    moved = jax.random.randint(jax.random.fold_in(key, 1), (twos,), 0, 1 << 20) % (room + 1)
    lengths = lengths.at[1:1 + 2 * twos:2].set(donor - moved).at[2:2 + 2 * twos:2].set(taker + moved)
    return lengths[jax.random.permutation(jax.random.fold_in(key, 2), amount)]


def gaussian(stream_key, dims, deviation, most, cuts=(), kind=jnp.bfloat16):
    loudness = shard_levels(stream_key, dims, cuts, -0.22, 0.18) if cuts else 1.0
    values = jax.random.normal(stream_key, dims, jnp.float32) * deviation * loudness
    return jnp.minimum(jnp.maximum(values, -most), most).astype(kind)


def setup_inputs(seed: int = 0) -> dict:
    key_list = jax.random.split(jax.random.key(seed), 12)
    return {
        "upper_out": gaussian(key_list[0], (TOKENS, MODEL_WIDTH), 1.0, 6.0, ((0, 512),)),
        "lower_out": gaussian(key_list[1], (TOKENS, MODEL_WIDTH), 1.0, 6.0, ((0, 512),)),
        "upper_grad": gaussian(key_list[2], (TOKENS, MODEL_WIDTH), 1.0, 6.0, ((0, 512),)),
        "lower_grad": gaussian(key_list[3], (TOKENS, MODEL_WIDTH), 1.0, 6.0, ((0, 512),)),
        "norm_gain": jnp.clip(1.0 + 0.1 * jax.random.normal(key_list[4], (MODEL_WIDTH,), jnp.float32), 0.5, 1.5),
        "query_weight": draw_query_weight(jax.random.fold_in(key_list[11], 71), 0),
        "key_weight": draw_key_weight(jax.random.fold_in(key_list[11], 71), 0),
        "value_matrix": gaussian(key_list[7], (MODEL_WIDTH, KEY_VALUE_HEADS * HEAD_WIDTH), MODEL_WIDTH ** -0.5, 0.125, ((0, 64),)),
        "out_weight": gaussian(key_list[8], (QUERY_HEADS * HEAD_WIDTH, MODEL_WIDTH), (QUERY_HEADS * HEAD_WIDTH) ** -0.5, 0.1875, ((0, 64),)),
        "route_table": jax.vmap(lambda own: jax.random.permutation(own, GROUPS))(jax.random.split(key_list[9], GROUPS * LANES)).reshape((GROUPS, LANES, GROUPS)).astype(jnp.int32),
        "doc_lengths": jax.vmap(lambda own: uneven_parts(own, DOCS, GROUP_ROWS, LONGEST, 2))(jax.random.split(key_list[10], GROUPS)).reshape((GROUPS, DOCS)).astype(jnp.int32),
    }


def attend(queries, out_grad, key_rows, value_rows, query_pos, doc_ids, block_rows, window, longest):
    count = queries.shape[0]
    grand_total = key_rows.shape[0]
    head_size = queries.shape[1]
    scale = 1.0 / math.sqrt(head_size)
    blocks = count // block_rows

    def step(carry, index):
        key_acc, value_acc = carry
        first = index * block_rows
        q_block = lax.dynamic_slice_in_dim(queries, first, block_rows, 0)
        g_block = lax.dynamic_slice_in_dim(out_grad, first, block_rows, 0)
        p_block = lax.dynamic_slice_in_dim(query_pos, first, block_rows, 0)
        start = jnp.clip(p_block[0] - longest + 1, 0, grand_total - window).astype(jnp.int32)
        k_win = lax.dynamic_slice_in_dim(key_rows, start, window, 0)
        v_win = lax.dynamic_slice_in_dim(value_rows, start, window, 0)
        d_win = lax.dynamic_slice_in_dim(doc_ids, start, window, 0)
        k_pos = start + jnp.arange(window, dtype=jnp.int32)
        q_doc = jnp.take(doc_ids, p_block)
        allowed = (d_win[None, :] == q_doc[:, None]) & (k_pos[None, :] <= p_block[:, None])
        scores = jnp.dot(q_block, k_win.T, preferred_element_type=jnp.float32) * scale
        scores = jnp.where(allowed, scores, -jnp.inf)
        peak = lax.optimization_barrier(jnp.max(scores, axis=1, keepdims=True))
        raised = jnp.exp(scores - peak)
        probs = raised / lax.optimization_barrier(jnp.sum(raised, axis=1, keepdims=True))
        prob_half = probs.astype(jnp.bfloat16)
        out_block = jnp.dot(prob_half, v_win, preferred_element_type=jnp.float32).astype(jnp.bfloat16)
        delta = lax.optimization_barrier(jnp.sum(g_block.astype(jnp.float32) * out_block.astype(jnp.float32), axis=1, keepdims=True))
        value_term = jnp.dot(prob_half.T, g_block, preferred_element_type=jnp.float32)
        prob_grad = jnp.dot(g_block, v_win.T, preferred_element_type=jnp.float32)
        score_grad = (probs * (prob_grad - delta)).astype(jnp.bfloat16)
        query_grad = (jnp.dot(score_grad, k_win, preferred_element_type=jnp.float32) * scale).astype(jnp.bfloat16)
        key_term = jnp.dot(score_grad.T, q_block, preferred_element_type=jnp.float32) * scale
        key_acc = lax.dynamic_update_slice_in_dim(key_acc, lax.dynamic_slice_in_dim(key_acc, start, window, 0) + key_term, start, 0)
        value_acc = lax.dynamic_update_slice_in_dim(value_acc, lax.dynamic_slice_in_dim(value_acc, start, window, 0) + value_term, start, 0)
        return ((key_acc, value_acc), (out_block, query_grad))
    zeros = jnp.zeros((grand_total, head_size), jnp.float32)
    (key_acc, value_acc), (outs, grads) = lax.scan(step, (zeros, zeros), jnp.arange(blocks, dtype=jnp.int32))
    return (outs.reshape(count, head_size), grads.reshape(count, head_size), key_acc, value_acc)

def reference(upper_out, lower_out, upper_grad, lower_grad, norm_gain, query_weight, key_weight, value_matrix, out_weight, route_table, doc_lengths):
    group_count = GROUPS
    lane_count = LANES
    piece_rows = TOK_DEV // group_count
    sequence_rows = lane_count * TOK_DEV
    length_classes = lane_count // QUERY_HEADS
    class_rows = TOK_DEV // length_classes
    query_count = lane_count * class_rows
    row_portion = QUERY_HEADS // KEY_VALUE_HEADS
    query_width = QUERY_HEADS * HEAD_WIDTH
    key_value_width = KEY_VALUE_HEADS * HEAD_WIDTH
    block_rows = min(512, query_count)
    window = min(sequence_rows, block_rows + LONGEST)
    lower_f = lower_out.astype(jnp.float32)
    inv_rms = lax.rsqrt(lax.optimization_barrier(jnp.mean(lower_f * lower_f, axis=1, keepdims=True)) + 1e-05)
    unit = lower_f * inv_rms
    normed = (unit * norm_gain.astype(jnp.float32)).astype(jnp.bfloat16)
    queries = jnp.dot(normed, query_weight, preferred_element_type=jnp.float32).astype(jnp.bfloat16)
    key_rows = jnp.dot(normed, key_weight, preferred_element_type=jnp.float32).astype(jnp.bfloat16)
    value_rows = jnp.dot(normed, value_matrix, preferred_element_type=jnp.float32).astype(jnp.bfloat16)
    out_grad = jnp.dot(upper_grad, out_weight.T, preferred_element_type=jnp.float32).astype(jnp.bfloat16)
    packed = jnp.concatenate([queries, out_grad, key_rows, value_rows], axis=1)
    width_all = packed.shape[1]
    pieces = packed.reshape(group_count, lane_count, group_count, piece_rows, width_all)
    targets = jnp.arange(group_count, dtype=jnp.int32)
    match = route_table[:, :, :, None] == targets[None, None, None, :]
    chosen = lax.optimization_barrier(jnp.sum(jnp.where(match, targets[None, None, :, None], 0), axis=2)).astype(jnp.int32)
    grouped = jnp.take_along_axis(pieces, chosen[:, :, :, None, None], axis=2)
    grouped = grouped.transpose(2, 1, 0, 3, 4).reshape(group_count, lane_count, length_classes, class_rows, width_all)
    grouped = grouped.transpose(0, 2, 1, 3, 4).reshape(group_count, sequence_rows, width_all)

    def per_group(item):
        gathered_rows, lens = item
        ends = jnp.cumsum(lens.astype(jnp.int32))
        positions = jnp.arange(sequence_rows, dtype=jnp.int32)
        doc_ids = lax.optimization_barrier(jnp.sum((ends[None, :] <= positions[:, None]).astype(jnp.int32), axis=1)).astype(jnp.int32)
        q_all = gathered_rows[:, :query_width]
        g_all = gathered_rows[:, query_width:2 * query_width]
        key_gathered = gathered_rows[:, 2 * query_width:2 * query_width + key_value_width].reshape(sequence_rows, KEY_VALUE_HEADS, HEAD_WIDTH).transpose(1, 0, 2)
        value_gathered = gathered_rows[:, 2 * query_width + key_value_width:].reshape(sequence_rows, KEY_VALUE_HEADS, HEAD_WIDTH).transpose(1, 0, 2)

        def by_head(array):
            return array.reshape(length_classes, query_count, QUERY_HEADS, HEAD_WIDTH).transpose(2, 0, 1, 3)
        q_heads = by_head(q_all)
        g_heads = by_head(g_all)
        owners = (jnp.arange(QUERY_HEADS, dtype=jnp.int32) // row_portion).astype(jnp.int32)

        def per_head(head_item):
            q_head, g_head, owner = head_item
            k_head = lax.dynamic_index_in_dim(key_gathered, owner, 0, keepdims=False)
            v_head = lax.dynamic_index_in_dim(value_gathered, owner, 0, keepdims=False)

            def per_class(class_item):
                q_class, g_class, klass = class_item
                query_pos = (klass * query_count + jnp.arange(query_count, dtype=jnp.int32)).astype(jnp.int32)
                outs, grads, key_acc, value_acc = attend(q_class, g_class, k_head, v_head, query_pos, doc_ids, block_rows, window, LONGEST)
                return (outs, grads, key_acc.astype(jnp.bfloat16), value_acc.astype(jnp.bfloat16))
            return lax.map(per_class, (q_head, g_head, jnp.arange(length_classes, dtype=jnp.int32)))
        outs, grads, key_parts, value_parts = lax.map(per_head, (q_heads, g_heads, owners))

        def to_rows(array):
            return array.transpose(1, 2, 0, 3).reshape(sequence_rows, query_width)

        def summed(part_count):
            grand_total = lax.optimization_barrier(jnp.sum(part_count.astype(jnp.float32).reshape(KEY_VALUE_HEADS, row_portion * length_classes, sequence_rows, HEAD_WIDTH), axis=1))
            return grand_total.astype(jnp.bfloat16).transpose(1, 0, 2).reshape(sequence_rows, key_value_width)
        return jnp.concatenate([to_rows(outs), to_rows(grads), summed(key_parts), summed(value_parts)], axis=1)
    home = lax.map(per_group, (grouped, doc_lengths))
    home = home.reshape(group_count, length_classes, lane_count, class_rows, width_all).transpose(0, 2, 1, 3, 4)
    home = home.reshape(group_count, lane_count, group_count, piece_rows, width_all).transpose(2, 1, 0, 3, 4)
    back = jnp.take_along_axis(home, route_table[:, :, :, None, None], axis=2).reshape(-1, width_all)
    attn_back = back[:, :query_width]
    query_back = back[:, query_width:2 * query_width]
    key_back = back[:, 2 * query_width:2 * query_width + key_value_width]
    value_back = back[:, 2 * query_width + key_value_width:]
    mixed = jnp.dot(attn_back, out_weight, preferred_element_type=jnp.float32)
    restored = (upper_out.astype(jnp.float32) - mixed).astype(jnp.bfloat16)
    normed_grad = jnp.dot(query_back, query_weight.T, preferred_element_type=jnp.float32)
    normed_grad = normed_grad + jnp.dot(key_back, key_weight.T, preferred_element_type=jnp.float32)
    normed_grad = normed_grad + jnp.dot(value_back, value_matrix.T, preferred_element_type=jnp.float32)
    unit_grad = normed_grad * norm_gain.astype(jnp.float32)
    lower_term = inv_rms * (unit_grad - unit * lax.optimization_barrier(jnp.mean(unit_grad * unit, axis=1, keepdims=True)))
    back_grad = (lower_grad.astype(jnp.float32) + lower_term).astype(jnp.bfloat16)
    return (restored, back_grad)
```

```python
import functools

import jax
import jax.numpy as jnp
from jax import lax
from jax.experimental import pallas as pl
from jax.experimental.pallas import tpu as pltpu
from jax.sharding import PartitionSpec as P

HEAD = 64
PAIR = 2 * HEAD
PIECE = 16
BLOCK = 512
TILE = 128
WINDOW = BLOCK + TILE
RING = 8
HEADS_KV = 4
GROUP_COLS = 4 * PAIR + PAIR
QKV_COLS = 4 * HEAD + PAIR
MESH = pl.DeviceIdType.MESH
F32 = jnp.float32
BF16 = jnp.bfloat16


def dot(a, b):
    return jnp.dot(a, b, preferred_element_type=F32)


def dot_nt(a, b):
    return lax.dot_general(a, b, (((1,), (1,)), ((), ())), preferred_element_type=F32)


def dot_tn(a, b):
    return lax.dot_general(a, b, (((0,), (0,)), ((), ())), preferred_element_type=F32)


class Place:
    def __init__(self):
        self.g = lax.axis_index("grp")
        self.s = lax.axis_index("sp")
        self.x, self.core = self.g // 2, self.g % 2
        self.z, self.y = self.s // RING, self.s % RING
        self.zp, self.zb = self.z // 2, self.z % 2
        self.block = self.x * 4 + self.zp
        self.a = self.y
        self.c = self.core + 2 * self.zb
        self.mine = self.c * 8 + self.a
        self.source = self.zb * 16 + self.y * 2 + self.core

    def attender(self, block, c, a):
        return {"grp": (block // 4) * 2 + c % 2, "sp": ((block % 4) * 2 + c // 2) * RING + a}

    def home(self, block, source):
        return {
            "grp": (block // 4) * 2 + source % 2,
            "sp": ((block % 4) * 2 + source // 16) * RING + (source // 2) % RING,
        }

    def after(self):
        return (self.block + 1) % 16

    def before(self):
        return (self.block + 15) % 16


def greet(at):
    barrier = pltpu.get_barrier_semaphore()

    def signal(device):
        pl.semaphore_signal(barrier, inc=1, device_id=device, device_id_type=MESH)

    for dz in (1, RING - 1):
        signal({"grp": at.g, "sp": ((at.z + dz) % RING) * RING + at.y})
    for d in range(1, 8):
        signal({"grp": (at.g + d) % 8, "sp": at.s})

    def own(d, carry):
        other = (at.mine + d) % 32
        signal(at.attender(at.block, other // 8, other % 8))
        return carry

    def both(d, carry):
        other = (at.mine + d) % 32
        signal(at.attender(at.after(), other // 8, other % 8))
        signal(at.attender(at.before(), other // 8, other % 8))
        return carry

    lax.fori_loop(1, 32, own, 0)
    lax.fori_loop(0, 32, both, 0)
    pl.semaphore_wait(barrier, 2 + 7 + 31 + 64)


class Gather:
    def __init__(self, at, full, sems):
        self.at, self.full = at, full
        self.out_sem, self.in_sem, self.share_out, self.share_in = sems
        self.count = 0
        self.pending = []

    def first_block(self, order, core, index, part):
        rows = slice(None) if part is None else pl.ds(PIECE * part, PIECE)
        j = 2 * core + order
        if order == 0:
            return self.full.at[j, self.at.z, index, rows]
        return self.full.at[j, index, self.at.y, rows]

    def second_block(self, order, core, index, part):
        j = 2 * core + order
        if order == 0:
            return self.full.at[j, index, pl.ds(4 * part, 4)]
        return self.full.at[j, pl.ds(4 * part, 4), index]

    def ring(self, order, phase, step):
        at = self.at
        if (order + phase) % 2 == 0:
            return {"grp": at.g, "sp": at.z * RING + (at.y + step) % RING}
        return {"grp": at.g, "sp": ((at.z + step) % RING) * RING + at.y}

    def position(self, order, phase):
        return self.at.y if (order + phase) % 2 == 0 else self.at.z

    def send(self, key, block, device):
        n = self.count
        self.count += 1
        copy = pltpu.make_async_remote_copy(
            src_ref=block, dst_ref=block, send_sem=self.out_sem.at[n], recv_sem=self.in_sem.at[n],
            device_id=device, device_id_type=MESH,
        )
        copy.start()
        self.pending.append((copy, n))
        return n

    def receive(self, n, block, sibling_block):
        at = self.at
        sibling = {"grp": at.x * 2 + 1 - at.core, "sp": at.s}
        pltpu.make_async_remote_copy(
            src_ref=block, dst_ref=block, send_sem=self.out_sem.at[n], recv_sem=self.in_sem.at[n],
            device_id=sibling, device_id_type=MESH,
        ).wait_recv()
        share = pltpu.make_async_remote_copy(
            src_ref=block, dst_ref=block, send_sem=self.share_out.at[n],
            recv_sem=self.share_in.at[n], device_id=sibling, device_id_type=MESH,
        )
        share.start()
        self.shares.append((share, n, sibling_block))

    def run(self, between):
        at = self.at
        self.shares = []
        for phase in (0, 1):
            slots = {}
            blocks = self.first_block if phase == 0 else self.second_block
            parts = (None,) if phase == 0 else (0, 1)
            for step in range(1, 6):
                for half, part in enumerate(parts):
                    for order in (0, 1):
                        here = self.position(order, phase)
                        for way in (1, -1):
                            def chunk(t):
                                if t < 4:
                                    return part
                                if phase == 0:
                                    return 0 if way == 1 else 1
                                return part if (part == 0) == (way == 1) else -1

                            if step > 1:
                                piece = chunk(step - 1)
                                if piece != -1:
                                    index = (here - way * (step - 1) + RING) % RING
                                    n = slots[(half, order, way, step - 1)]
                                    self.receive(
                                        n,
                                        blocks(order, at.core, index, piece),
                                        blocks(order, 1 - at.core, index, piece),
                                    )
                            if step < 5:
                                piece = chunk(step)
                                if piece != -1:
                                    index = (here - way * (step - 1) + RING) % RING
                                    slots[(half, order, way, step)] = self.send(
                                        None,
                                        blocks(order, at.core, index, piece),
                                        self.ring(order, phase, way),
                                    )
                if phase == 0 and step == 1:
                    between()

    def shared(self):
        for share, n, block in self.shares:
            pltpu.make_async_copy(block, block, self.share_in.at[n]).wait()

    def drain(self):
        for copy, _ in self.pending:
            copy.wait_send()
        for share, _, _ in self.shares:
            share.wait_send()


def attention(at, recv, halo, keys, total, back, ends_ref):
    low = lax.broadcasted_iota(jnp.int32, (1, PAIR), 1) < HEAD
    pick_query = jnp.where(low, 0.125, 0.0).astype(BF16)
    pick_grad = jnp.where(low, 0.0, 1.0).astype(BF16)
    low_rows = lax.broadcasted_iota(jnp.int32, (PAIR, TILE), 0) < HEAD
    keys[pl.ds(0, BLOCK), :] = halo[...]
    keys[pl.ds(BLOCK, BLOCK), :] = recv[:, 4 * PAIR :]
    total[...] = jnp.zeros_like(total)
    ends = ends_ref[...]

    def tile(t, carry):
        first = pl.multiple_of(t * TILE, TILE)
        both = jnp.concatenate(
            [recv[pl.ds(first, TILE), PAIR * h : PAIR * (h + 1)] for h in range(4)], axis=0
        )
        queries = both * pick_query
        grads = both * pick_grad
        window = keys[pl.ds(first, WINDOW), :]
        window_t = window.T
        scores = dot_nt(window, queries)
        prob_grad = dot_nt(window, grads)
        position = at.block * BLOCK + first + lax.broadcasted_iota(jnp.int32, (1, TILE), 1)
        began = jnp.max(jnp.where(ends <= position, ends, 0), axis=0, keepdims=True)
        key_position = (at.block - 1) * BLOCK + first + lax.broadcasted_iota(
            jnp.int32, (WINDOW, TILE), 0
        )
        allowed = (key_position >= began) & (key_position <= position)
        halves, slopes = [], []
        for h in range(4):
            cols = slice(TILE * h, TILE * (h + 1))
            s = jnp.where(allowed, scores[:, cols], -jnp.inf)
            raised = jnp.exp(s - jnp.max(s, axis=0, keepdims=True))
            probs = raised * (1.0 / jnp.sum(raised, axis=0, keepdims=True))
            half = probs.astype(BF16)
            out_t = dot(window_t, half).astype(BF16).astype(F32)
            grad_t = grads[cols, :].astype(F32).T
            delta = jnp.sum(grad_t * out_t, axis=0, keepdims=True)
            slope = (probs * (prob_grad[:, cols] - delta)).astype(BF16)
            query_grad = dot(window_t, slope) * 0.125
            result = jnp.where(low_rows, query_grad, out_t).T.astype(BF16)
            back[pl.ds(first, TILE), PAIR * h : PAIR * (h + 1)] = result
            halves.append(half)
            slopes.append(slope)
        total[pl.ds(first, WINDOW), :] += dot(
            jnp.concatenate(slopes, axis=1), queries
        ) + dot(jnp.concatenate(halves, axis=1), grads)
        return carry

    lax.fori_loop(0, BLOCK // TILE, tile, 0)
    back[:, 4 * PAIR :] = total[pl.ds(BLOCK, BLOCK), :].astype(BF16)


def swap_halves(a):
    return pltpu.roll(a, HEAD, 1)


def kernel(
    lower_ref, ugrad_ref, uout_ref, lgrad_ref, gain_ref, shard_ref, dest_ref, ends_in,
    restored_ref, backg_ref,
    full, normed, send, recv, halo, keys, total, back, back_halo, ret, ret_halo, ends,
    g_out, g_in, h_out, h_in, sems,
):
    at = Place()
    rows = lower_ref.shape[0]
    greet(at)

    @pl.when(at.y == at.g)
    def _():
        def tell(d, carry):
            pltpu.make_async_remote_copy(
                src_ref=ends_in, dst_ref=ends, send_sem=sems.at[0], recv_sem=sems.at[1],
                device_id={"grp": (at.g + d) % 8, "sp": at.s}, device_id_type=MESH,
            ).start()
            return carry

        lax.fori_loop(1, 8, tell, 0)
        ends[...] = ends_in[...]

    for j in range(HEADS_KV):
        full[j, at.z, at.y] = shard_ref[j]

    def inverse_rms():
        low = lower_ref[...].astype(F32)
        return low, lax.rsqrt(jnp.mean(low * low, axis=1, keepdims=True) + 1e-05)

    def norm():
        low, inv = inverse_rms()
        normed[...] = ((low * inv) * gain_ref[...]).astype(BF16)

    gather = Gather(at, full, (g_out, g_in, h_out, h_in))
    gather.run(norm)
    gather.shared()

    def out_half(j, h):
        return full[j, :, :, PIECE * h : PIECE * (h + 1), QKV_COLS:].reshape(
            QUERY_COLS, GROUP_COLS - QKV_COLS
        )

    QUERY_COLS = HEADS_KV * 4 * HEAD
    deep = RING * RING * 32
    permute = (
        lax.broadcasted_iota(jnp.int32, (rows, rows), 0) == dest_ref[...]
    ).astype(F32).astype(BF16)
    low = lax.broadcasted_iota(jnp.int32, (rows, PAIR), 1) < HEAD

    grad_cols = jnp.zeros((rows, QUERY_COLS), F32)
    for j in range(HEADS_KV):
        for h in range(2):
            first = 512 * j + 256 * h
            grad_cols = grad_cols + dot_nt(ugrad_ref[:, first : first + 256], out_half(j, h))
    for c in range(HEADS_KV):
        qkv = dot(normed[...], full[c, :, :, :, :QKV_COLS].reshape(deep, QKV_COLS))
        parts = []
        for p in range(2):
            q2 = qkv[:, PAIR * p : PAIR * (p + 1)]
            g2 = grad_cols[:, 256 * c + PAIR * p : 256 * c + PAIR * (p + 1)]
            parts.append(jnp.where(low, q2, swap_halves(g2)).astype(BF16))
            parts.append(jnp.where(low, swap_halves(q2), g2).astype(BF16))
        parts.append(qkv[:, 4 * HEAD :].astype(BF16))
        send[c] = dot(permute, jnp.concatenate(parts, axis=1)).astype(BF16)

    def piece(i):
        return pl.ds(pl.multiple_of(i * PIECE, PIECE), PIECE)

    kv_cols = pl.ds(4 * PAIR, PAIR)
    local = pltpu.make_async_copy(
        send.at[at.c, piece(at.a), :], recv.at[piece(at.source), :], sems.at[3]
    )
    local.start()

    def send_own(d, carry):
        other = (at.mine + d) % 32
        c, a = other // 8, other % 8
        pltpu.make_async_remote_copy(
            src_ref=send.at[c, piece(a), :], dst_ref=recv.at[piece(at.source), :],
            send_sem=sems.at[2], recv_sem=sems.at[3],
            device_id=at.attender(at.block, c, a), device_id_type=MESH,
        ).start()
        return carry

    def send_halo(d, carry):
        other = (at.mine + d) % 32
        c, a = other // 8, other % 8
        pltpu.make_async_remote_copy(
            src_ref=send.at[c, piece(a), kv_cols], dst_ref=halo.at[piece(at.source), :],
            send_sem=sems.at[4], recv_sem=sems.at[5],
            device_id=at.attender(at.after(), c, a), device_id_type=MESH,
        ).start()
        return carry

    lax.fori_loop(0, 32, send_halo, 0)
    lax.fori_loop(1, 32, send_own, 0)

    def wait_bytes(ref, sem):
        pltpu.make_async_copy(ref, ref, sem).wait()

    @pl.when(at.y != at.g)
    def _():
        wait_bytes(ends, sems.at[1])

    wait_bytes(halo, sems.at[5])
    wait_bytes(recv, sems.at[3])
    attention(at, recv, halo, keys, total, back, ends)
    back_halo[...] = total[pl.ds(0, BLOCK), :].astype(BF16)

    local_back = pltpu.make_async_copy(
        back.at[piece(at.source), :], ret.at[at.c, piece(at.a), :], sems.at[7]
    )
    local_back.start()

    def return_own(d, carry):
        source = (at.source + d) % 32
        pltpu.make_async_remote_copy(
            src_ref=back.at[piece(source), :], dst_ref=ret.at[at.c, piece(at.a), :],
            send_sem=sems.at[6], recv_sem=sems.at[7],
            device_id=at.home(at.block, source), device_id_type=MESH,
        ).start()
        return carry

    def return_halo(d, carry):
        source = (at.source + d) % 32
        pltpu.make_async_remote_copy(
            src_ref=back_halo.at[piece(source), :], dst_ref=ret_halo.at[at.c, piece(at.a), :],
            send_sem=sems.at[8], recv_sem=sems.at[9],
            device_id=at.home(at.before(), source), device_id_type=MESH,
        ).start()
        return carry

    lax.fori_loop(0, 32, return_halo, 0)
    lax.fori_loop(1, 32, return_own, 0)
    wait_bytes(ret_halo, sems.at[9])
    wait_bytes(ret, sems.at[7])

    normed_grad = jnp.zeros((rows, deep), F32)
    attended = []
    for c in range(HEADS_KV):
        got = ret[c]
        kv = (got[:, 4 * PAIR :].astype(F32) + ret_halo[c].astype(F32)).astype(BF16)
        mine = dot_tn(permute, jnp.concatenate([got[:, : 4 * PAIR], kv], axis=1))
        slopes = []
        for p in range(2):
            even = mine[:, 2 * PAIR * p : 2 * PAIR * p + PAIR]
            odd = mine[:, 2 * PAIR * p + PAIR : 2 * PAIR * (p + 1)]
            slopes.append(jnp.where(low, even, swap_halves(odd)).astype(BF16))
            attended.append(jnp.where(low, swap_halves(even), odd).astype(BF16))
        slopes.append(mine[:, 4 * PAIR :].astype(BF16))
        normed_grad = normed_grad + dot_nt(
            jnp.concatenate(slopes, axis=1),
            full[c, :, :, :, :QKV_COLS].reshape(deep, QKV_COLS),
        )
    attended = jnp.concatenate(attended, axis=1)
    for j in range(HEADS_KV):
        for h in range(2):
            first = 512 * j + 256 * h
            mixed = dot(attended, out_half(j, h))
            restored_ref[:, first : first + 256] = (
                uout_ref[:, first : first + 256].astype(F32) - mixed
            ).astype(BF16)
    low_f, inv = inverse_rms()
    unit = low_f * inv
    unit_grad = normed_grad * gain_ref[...]
    term = inv * (unit_grad - unit * jnp.mean(unit_grad * unit, axis=1, keepdims=True))
    backg_ref[...] = (lgrad_ref[...].astype(F32) + term).astype(BF16)

    gather.drain()
    wait_bytes(recv.at[pl.ds(0, 31 * PIECE), :], sems.at[2])
    wait_bytes(halo, sems.at[4])
    wait_bytes(recv.at[pl.ds(0, 31 * PIECE), :], sems.at[6])
    wait_bytes(halo, sems.at[8])

    @pl.when(at.y == at.g)
    def _():
        wait_bytes(halo.at[pl.ds(0, 448), :], sems.at[0])


def per_device(
    upper_out, lower_out, upper_grad, lower_grad, norm_gain, query_weight, key_weight,
    value_matrix, out_weight, route_table, doc_lengths,
):
    rows, width = lower_out.shape
    shard = []
    for j in range(HEADS_KV):
        q = query_weight[:, 256 * j : 256 * (j + 1)]
        k = key_weight[:, HEAD * j : HEAD * (j + 1)]
        v = value_matrix[:, HEAD * j : HEAD * (j + 1)]
        o = out_weight[:, 512 * j : 512 * (j + 1)]
        o = jnp.concatenate([o[:, :256], o[:, 256:]], axis=0)
        shard.append(jnp.concatenate([q, k, v, o], axis=1))
    shard = jnp.stack(shard)
    routed = jnp.repeat(route_table.reshape(-1), PIECE) * PIECE
    dest = (routed + jnp.arange(rows, dtype=jnp.int32) % PIECE).reshape(1, rows)
    lens = doc_lengths.reshape(-1)
    docs = lens.shape[0]
    order = jnp.arange(docs, dtype=jnp.int32)
    ends = jnp.sum(jnp.where(order[None, :] <= order[:, None], lens[None, :], 0), axis=1)
    ends = jnp.broadcast_to(ends[:, None], (docs, TILE))

    vmem = pl.BlockSpec(memory_space=pltpu.VMEM)
    dma = pltpu.SemaphoreType.DMA
    return pl.pallas_call(
        kernel,
        out_shape=(jax.ShapeDtypeStruct((rows, width), BF16),) * 2,
        in_specs=[vmem] * 8,
        out_specs=(vmem, vmem),
        scratch_shapes=[
            pltpu.VMEM((HEADS_KV, RING, RING, 32, GROUP_COLS), BF16),
            pltpu.VMEM((rows, width), BF16),
            pltpu.VMEM((HEADS_KV, rows, GROUP_COLS), BF16),
            pltpu.VMEM((BLOCK, GROUP_COLS), BF16),
            pltpu.VMEM((BLOCK, PAIR), BF16),
            pltpu.VMEM((2 * BLOCK, PAIR), BF16),
            pltpu.VMEM((2 * BLOCK, PAIR), F32),
            pltpu.VMEM((BLOCK, GROUP_COLS), BF16),
            pltpu.VMEM((BLOCK, PAIR), BF16),
            pltpu.VMEM((HEADS_KV, rows, GROUP_COLS), BF16),
            pltpu.VMEM((HEADS_KV, rows, PAIR), BF16),
            pltpu.VMEM((docs, TILE), jnp.int32),
            dma((48,)), dma((48,)), dma((48,)), dma((48,)), dma((10,)),
        ],
        compiler_params=pltpu.CompilerParams(
            collective_id=0, has_side_effects=True, vmem_limit_bytes=56 * 1024 * 1024
        ),
        name="coupling",
    )(
        lower_out, upper_grad, upper_out, lower_grad, norm_gain.reshape(1, width), shard, dest, ends
    )


def solution(mesh):
    rows = P(("grp", "sp"), None)
    return jax.shard_map(
        per_device,
        mesh=mesh,
        in_specs=(
            rows, rows, rows, rows, P(), P("sp", None), P("sp", None), P("sp", None),
            P("sp", None), P("grp", "sp", None), P("grp", None),
        ),
        out_specs=(rows, rows),
        check_vma=False,
    )
```

```python
import functools

import jax
import jax.numpy as jnp
from jax import lax
from jax.experimental import pallas as pl
from jax.experimental.pallas import tpu as pltpu
from jax.sharding import PartitionSpec as P

HEAD = 64
PAIR = 2 * HEAD
PIECE = 16
BLOCK = 512
TILE = 128
WINDOW = BLOCK + TILE
RING = 8
HEADS_KV = 4
GROUP_COLS = 4 * PAIR + PAIR
QKV_COLS = 4 * HEAD + PAIR
MESH = pl.DeviceIdType.MESH
F32 = jnp.float32
BF16 = jnp.bfloat16


def dot(a, b):
    return jnp.dot(a, b, preferred_element_type=F32)


def dot_nt(a, b):
    return lax.dot_general(a, b, (((1,), (1,)), ((), ())), preferred_element_type=F32)


def dot_tn(a, b):
    return lax.dot_general(a, b, (((0,), (0,)), ((), ())), preferred_element_type=F32)


class Place:
    def __init__(self):
        self.g = lax.axis_index("grp")
        self.s = lax.axis_index("sp")
        self.x, self.core = self.g // 2, self.g % 2
        self.z, self.y = self.s // RING, self.s % RING
        self.zp, self.zb = self.z // 2, self.z % 2
        self.block = self.x * 4 + self.zp
        self.a = self.y
        self.c = self.core + 2 * self.zb
        self.mine = self.c * 8 + self.a
        self.source = self.zb * 16 + self.y * 2 + self.core

    def attender(self, block, c, a):
        return {"grp": (block // 4) * 2 + c % 2, "sp": ((block % 4) * 2 + c // 2) * RING + a}

    def home(self, block, source):
        return {
            "grp": (block // 4) * 2 + source % 2,
            "sp": ((block % 4) * 2 + source // 16) * RING + (source // 2) % RING,
        }

    def after(self):
        return (self.block + 1) % 16

    def before(self):
        return (self.block + 15) % 16


def greet(at):
    barrier = pltpu.get_barrier_semaphore()

    def signal(device):
        pl.semaphore_signal(barrier, inc=1, device_id=device, device_id_type=MESH)

    for dz in (1, RING - 1):
        signal({"grp": at.g, "sp": ((at.z + dz) % RING) * RING + at.y})
    signal(at.attender(at.after(), at.c, at.a))
    signal(at.attender(at.before(), at.c, at.a))

    def column(d, carry):
        signal({"grp": (at.g + d) % 8, "sp": at.s})
        return carry

    def own(d, carry):
        other = (at.mine + d) % 32
        signal(at.attender(at.block, other // 8, other % 8))
        return carry

    lax.fori_loop(1, 8, column, 0)
    lax.fori_loop(1, 32, own, 0)
    pl.semaphore_wait(barrier, 2 + 2 + 7 + 31)


def wait_bytes(ref, sem):
    pltpu.make_async_copy(ref, ref, sem).wait()


class Gather:
    def __init__(self, at, full, sems):
        self.at, self.full = at, full
        self.first_in, self.second_in, self.share_in, self.out = sems
        self.spot = ((at.y, at.z), (at.z, at.y))

    def shard(self, order, core, i1, i2, half):
        z, y = (i2, i1) if order == 0 else (i1, i2)
        rows = slice(None) if half is None else pl.ds(PIECE * half, PIECE)
        return self.full.at[2 * core + order, z, y, rows]

    def line(self, order, core, i2):
        j = 2 * core + order
        return self.full.at[j, i2] if order == 0 else self.full.at[j, :, i2]

    def step(self, order, axis, way):
        at = self.at
        if (order + axis) % 2 == 0:
            return {"grp": at.g, "sp": at.z * RING + (at.y + way + RING) % RING}
        return {"grp": at.g, "sp": ((at.z + way + RING) % RING) * RING + at.y}

    def first(self, order, way, t, i1):
        half = None if t < 4 else (1 - way) // 2
        block = self.shard(order, self.at.core, i1, self.spot[order][1], half)
        return pltpu.make_async_remote_copy(
            src_ref=block, dst_ref=block, send_sem=self.out.at[order],
            recv_sem=self.first_in.at[order, (1 - way) // 2, t - 1],
            device_id=self.step(order, 0, way), device_id_type=MESH,
        )

    def second(self, order, way, k, m, i2):
        half = None if m < 4 else (1 - way) // 2
        i1 = (self.spot[order][0] + k + RING) % RING
        block = self.shard(order, self.at.core, i1, i2, half)
        return pltpu.make_async_remote_copy(
            src_ref=block, dst_ref=block, send_sem=self.out.at[2 + order],
            recv_sem=self.second_in.at[order, (1 - way) // 2, (k + RING) % RING, m - 1],
            device_id=self.step(order, 1, way), device_id_type=MESH,
        )

    def share(self, order, n, block):
        at = self.at
        return pltpu.make_async_remote_copy(
            src_ref=block, dst_ref=block, send_sem=self.out.at[4 + (n >= 7) * 2 + order],
            recv_sem=self.share_in.at[order, n],
            device_id={"grp": at.x * 2 + 1 - at.core, "sp": at.s}, device_id_type=MESH,
        )

    def share_block(self, order, core, n):
        p1, p2 = self.spot[order]
        if n < 7:
            return self.shard(order, core, (p1 + n + 1) % RING, p2, None)
        return self.line(order, core, (p2 + n - 6) % RING)

    def hand_over(self, order, n):
        self.share(order, n, self.share_block(order, self.at.core, n)).start()

    def run(self, filler):
        for tick in range(9):
            for order in (0, 1):
                p1 = self.spot[order][0]
                for way in (1, -1):
                    if 1 <= tick <= 4:
                        i1 = (p1 - way * tick + RING) % RING
                        self.first(order, way, tick, i1).wait_recv()
                        if tick < 4:
                            self.hand_over(order, (-way * tick) % RING - 1)
                    if tick < 4:
                        i1 = (p1 - way * tick + RING) % RING
                        self.first(order, way, tick + 1, i1).start()
                if tick == 4:
                    self.hand_over(order, 3)
            for k in (4, 3, -3, 2, -2, 1, -1, 0):
                m = tick - abs(k) + 1
                if m < 1 or m > 5:
                    continue
                for order in (0, 1):
                    p2 = self.spot[order][1]
                    for way in (1, -1):
                        i2 = (p2 - way * (m - 1) + RING) % RING
                        if m > 1:
                            self.second(order, way, k, m - 1, i2).wait_recv()
                        if m < 5:
                            self.second(order, way, k, m, i2).start()
                        if k == 4 and 1 < m < 5:
                            self.hand_over(order, 7 + (-way * (m - 1)) % RING - 1)
                    if k == 4 and m == 5:
                        self.hand_over(order, 10)
                next(filler, None)
        for _ in filler:
            pass
        for order in (0, 1):
            for n in range(14):
                wait_bytes(
                    self.share_block(order, 1 - self.at.core, n), self.share_in.at[order, n]
                )

    def drain(self):
        for order in (0, 1):
            wait_bytes(self.full.at[0, 0, pl.ds(0, 7)], self.out.at[order])
            wait_bytes(self.full.at[0, pl.ds(0, 7)], self.out.at[2 + order])
            wait_bytes(self.full.at[0, 0, pl.ds(0, 7)], self.out.at[4 + order])
            wait_bytes(self.full.at[0, pl.ds(0, 7)], self.out.at[6 + order])


def attention(at, pair, recv, keys, total, back, ends_ref, finish):
    low = lax.broadcasted_iota(jnp.int32, (1, PAIR), 1) < HEAD
    pick_query = jnp.where(low, 0.125, 0.0).astype(BF16)
    pick_grad = jnp.where(low, 0.0, 1.0).astype(BF16)
    low_rows = lax.broadcasted_iota(jnp.int32, (PAIR, TILE), 0) < HEAD
    ends = ends_ref[...]
    heads = (2 * pair, 2 * pair + 1)

    def tile(t, carry):
        first = pl.multiple_of(t * TILE, TILE)
        both = jnp.concatenate(
            [recv[pl.ds(first, TILE), PAIR * h : PAIR * (h + 1)] for h in heads], axis=0
        )
        queries = both * pick_query
        grads = both * pick_grad
        window = keys[pl.ds(first, WINDOW), :]
        window_t = window.T
        scores = dot_nt(window, queries)
        prob_grad = dot_nt(window, grads)
        position = at.block * BLOCK + first + lax.broadcasted_iota(jnp.int32, (1, TILE), 1)
        began = jnp.max(jnp.where(ends <= position, ends, 0), axis=0, keepdims=True)
        key_position = (at.block - 1) * BLOCK + first + lax.broadcasted_iota(
            jnp.int32, (WINDOW, TILE), 0
        )
        allowed = (key_position >= began) & (key_position <= position)
        halves, slopes = [], []
        for i, h in enumerate(heads):
            cols = slice(TILE * i, TILE * (i + 1))
            s = jnp.where(allowed, scores[:, cols], -jnp.inf)
            raised = jnp.exp(s - jnp.max(s, axis=0, keepdims=True))
            probs = raised * (1.0 / jnp.sum(raised, axis=0, keepdims=True))
            half = probs.astype(BF16)
            out_t = dot(window_t, half).astype(BF16).astype(F32)
            grad_t = grads[cols, :].astype(F32).T
            delta = jnp.sum(grad_t * out_t, axis=0, keepdims=True)
            slope = (probs * (prob_grad[:, cols] - delta)).astype(BF16)
            query_grad = dot(window_t, slope) * 0.125
            result = jnp.where(low_rows, query_grad, out_t).T.astype(BF16)
            back[pl.ds(first, TILE), PAIR * h : PAIR * (h + 1)] = result
            halves.append(half)
            slopes.append(slope)
        total[pl.ds(first, WINDOW), :] += dot(
            jnp.concatenate(slopes, axis=1), queries
        ) + dot(jnp.concatenate(halves, axis=1), grads)
        finish(first)
        return carry

    lax.fori_loop(0, BLOCK // TILE, tile, 0)


def swap_halves(a):
    return pltpu.roll(a, HEAD, 1)


def kernel(
    lower_hbm, ugrad_hbm, uout_hbm, lgrad_hbm, gain_ref, wq_ref, wk_ref, wv_ref, wo_ref,
    route_ref, lens_ref,
    restored_hbm, backg_hbm,
    lower_ref, ugrad_ref, uout_ref, lgrad_ref, restored_ref, backg_ref,
    full, normed, send, recv, keys, total, back, back_halo, halo_grad, ret, ends_own, ends,
    first_in, second_in, share_in, gather_out, sems, local_sems,
):
    at = Place()
    rows, width = lower_ref.shape
    deep = RING * RING * 32
    query_cols = HEADS_KV * 4 * HEAD
    low = lax.broadcasted_iota(jnp.int32, (rows, PAIR), 1) < HEAD
    loads = [
        pltpu.make_async_copy(src, dst, local_sems.at[n])
        for n, (src, dst) in enumerate(
            ((lower_hbm, lower_ref), (ugrad_hbm, ugrad_ref), (uout_hbm, uout_ref),
             (lgrad_hbm, lgrad_ref))
        )
    ]
    for load in loads:
        load.start()

    low_w = lax.broadcasted_iota(jnp.int32, (32, PAIR), 1) < HEAD
    for j in range(HEADS_KV):
        full[j, at.z, at.y, :, : 4 * HEAD] = wq_ref[:, 256 * j : 256 * (j + 1)]
        k2 = wk_ref[:, PAIR * (j // 2) : PAIR * (j // 2 + 1)].astype(F32)
        v2 = wv_ref[:, PAIR * (j // 2) : PAIR * (j // 2 + 1)].astype(F32)
        if j % 2 == 0:
            kv = jnp.where(low_w, k2, swap_halves(v2))
        else:
            kv = jnp.where(low_w, swap_halves(k2), v2)
        full[j, at.z, at.y, :, 4 * HEAD : QKV_COLS] = kv.astype(BF16)
        for h in range(2):
            first = 512 * j + 256 * h
            full[j, at.z, at.y, PIECE * h : PIECE * (h + 1), QKV_COLS:] = wo_ref[
                :, first : first + 256
            ]
    docs = ends.shape[0]
    doc = lax.broadcasted_iota(jnp.int32, (docs, TILE), 0)
    until = jnp.zeros((docs, TILE), jnp.int32)
    so_far = 0
    for k in range(docs):
        so_far = so_far + lens_ref[0, k]
        until = jnp.where(doc == k, so_far, until)
    ends_own[...] = until
    greet(at)

    @pl.when(at.y == at.g)
    def _():
        def tell(d, carry):
            pltpu.make_async_remote_copy(
                src_ref=ends_own, dst_ref=ends, send_sem=sems.at[0], recv_sem=sems.at[1],
                device_id={"grp": (at.g + d) % 8, "sp": at.s}, device_id_type=MESH,
            ).start()
            return carry

        lax.fori_loop(1, 8, tell, 0)
        ends[...] = ends_own[...]

    def norm():
        loads[0].wait()
        for r in range(0, rows, PIECE):
            part = lower_ref[r : r + PIECE, :].astype(F32)
            inv = lax.rsqrt(jnp.mean(part * part, axis=1, keepdims=True) + 1e-05)
            normed[r : r + PIECE, :] = ((part * inv) * gain_ref[...]).astype(BF16)
            yield

    gather = Gather(at, full, (first_in, second_in, share_in, gather_out))
    gather.run(norm())
    loads[1].wait()

    def out_half(j, h):
        return full[j, :, :, PIECE * h : PIECE * (h + 1), QKV_COLS:].reshape(
            query_cols, GROUP_COLS - QKV_COLS
        )

    def piece(i):
        return pl.ds(pl.multiple_of(i * PIECE, PIECE), PIECE)

    columns = (pl.ds(0, 2 * PAIR), pl.ds(2 * PAIR, 2 * PAIR), pl.ds(4 * PAIR, PAIR))

    def put_out(part):
        cols = columns[part]

        def target(source):
            if part == 2:
                return keys.at[pl.ds(pl.multiple_of(BLOCK + source * PIECE, PIECE), PIECE), :]
            return recv.at[piece(source), cols]

        pltpu.make_async_copy(
            send.at[at.c, piece(at.a), cols], target(at.source), sems.at[4 + part]
        ).start()

        def one(d, carry):
            other = (at.mine + d) % 32
            c, a = other // 8, other % 8
            pltpu.make_async_remote_copy(
                src_ref=send.at[c, piece(a), cols], dst_ref=target(at.source),
                send_sem=sems.at[10 + part], recv_sem=sems.at[4 + part],
                device_id=at.attender(at.block, c, a), device_id_type=MESH,
            ).start()
            return carry

        lax.fori_loop(1, 32, one, 0)

    def put_back(part):
        cols = columns[part]
        pltpu.make_async_copy(
            back.at[piece(at.source), cols], ret.at[at.c, piece(at.a), cols], sems.at[7 + part]
        ).start()

        def one(d, carry):
            source = (at.source + d) % 32
            pltpu.make_async_remote_copy(
                src_ref=back.at[piece(source), cols], dst_ref=ret.at[at.c, piece(at.a), cols],
                send_sem=sems.at[13 + part], recv_sem=sems.at[7 + part],
                device_id=at.home(at.block, source), device_id_type=MESH,
            ).start()
            return carry

        lax.fori_loop(1, 32, one, 0)

    row = lax.broadcasted_iota(jnp.int32, (1, rows), 1)
    dest = row % PIECE
    for p in range(rows // PIECE):
        dest = jnp.where(row // PIECE == p, dest + route_ref[0, 0, p] * PIECE, dest)
    permute = (
        lax.broadcasted_iota(jnp.int32, (rows, rows), 0) == dest
    ).astype(F32).astype(BF16)

    query_parts = []
    for c in range(HEADS_KV):
        qkv = dot(normed[...], full[c, :, :, :, :QKV_COLS].reshape(deep, QKV_COLS))
        query_parts.append(qkv[:, : 4 * HEAD])
        send[c, :, 4 * PAIR :] = dot(permute, qkv[:, 4 * HEAD :].astype(BF16)).astype(BF16)
    put_out(2)
    grad_cols = jnp.zeros((rows, query_cols), F32)
    for j in range(HEADS_KV):
        for h in range(2):
            first = 512 * j + 256 * h
            grad_cols = grad_cols + dot_nt(ugrad_ref[:, first : first + 256], out_half(j, h))
    for p in range(2):
        for c in range(HEADS_KV):
            q2 = query_parts[c][:, PAIR * p : PAIR * (p + 1)]
            g2 = grad_cols[:, 256 * c + PAIR * p : 256 * c + PAIR * (p + 1)]
            message = jnp.concatenate(
                [
                    jnp.where(low, q2, swap_halves(g2)).astype(BF16),
                    jnp.where(low, swap_halves(q2), g2).astype(BF16),
                ],
                axis=1,
            )
            send[c, :, 2 * PAIR * p : 2 * PAIR * (p + 1)] = dot(permute, message).astype(BF16)
        put_out(p)

    own_keys, old_keys = keys.at[pl.ds(BLOCK, BLOCK), :], keys.at[pl.ds(0, BLOCK), :]
    wait_bytes(own_keys, sems.at[6])
    hand_on = pltpu.make_async_remote_copy(
        src_ref=own_keys, dst_ref=old_keys, send_sem=sems.at[2], recv_sem=sems.at[3],
        device_id=at.attender(at.after(), at.c, at.a), device_id_type=MESH,
    )
    hand_on.start()
    total[...] = jnp.zeros_like(total)

    @pl.when(at.y != at.g)
    def _():
        wait_bytes(ends, sems.at[1])

    hand_on.wait_recv()

    def hand_back(first):
        done = pl.ds(first, TILE)
        back_halo[done, :] = total[done, :].astype(BF16)
        pltpu.make_async_remote_copy(
            src_ref=back_halo.at[done, :], dst_ref=halo_grad.at[done, :], send_sem=sems.at[16],
            recv_sem=sems.at[17], device_id=at.attender(at.before(), at.c, at.a),
            device_id_type=MESH,
        ).start()

    for p in range(2):
        wait_bytes(recv.at[:, columns[p]], sems.at[4 + p])
        attention(at, p, recv, keys, total, back, ends, hand_back if p else lambda first: None)
        put_back(p)
    wait_bytes(halo_grad, sems.at[17])
    back[:, 4 * PAIR :] = (total[pl.ds(BLOCK, BLOCK), :] + halo_grad[...].astype(F32)).astype(BF16)
    put_back(2)

    normed_grad = jnp.zeros((rows, deep), F32)
    attended, slopes = [[] for _ in range(2)], [[] for _ in range(HEADS_KV)]
    for p in range(2):
        wait_bytes(ret.at[:, :, columns[p]], sems.at[7 + p])
        for c in range(HEADS_KV):
            mine = dot_tn(permute, ret[c, :, 2 * PAIR * p : 2 * PAIR * (p + 1)])
            even, odd = mine[:, :PAIR], mine[:, PAIR:]
            slopes[c].append(jnp.where(low, even, swap_halves(odd)).astype(BF16))
            attended[p].append(jnp.where(low, swap_halves(even), odd).astype(BF16))
    both = jnp.concatenate([attended[p][c] for c in range(HEADS_KV) for p in range(2)], axis=1)
    loads[2].wait()
    for j in range(HEADS_KV):
        for h in range(2):
            first = 512 * j + 256 * h
            mixed = dot(both, out_half(j, h))
            restored_ref[:, first : first + 256] = (
                uout_ref[:, first : first + 256].astype(F32) - mixed
            ).astype(BF16)
    store = pltpu.make_async_copy(restored_ref, restored_hbm, local_sems.at[4])
    store.start()
    wait_bytes(ret.at[:, :, columns[2]], sems.at[9])
    for c in range(HEADS_KV):
        slopes[c].append(dot_tn(permute, ret[c, :, 4 * PAIR :]).astype(BF16))
        normed_grad = normed_grad + dot_nt(
            jnp.concatenate(slopes[c], axis=1),
            full[c, :, :, :, :QKV_COLS].reshape(deep, QKV_COLS),
        )
    loads[3].wait()
    low_f = lower_ref[...].astype(F32)
    inv = lax.rsqrt(jnp.mean(low_f * low_f, axis=1, keepdims=True) + 1e-05)
    unit = low_f * inv
    unit_grad = normed_grad * gain_ref[...]
    term = inv * (unit_grad - unit * jnp.mean(unit_grad * unit, axis=1, keepdims=True))
    backg_ref[...] = (lgrad_ref[...].astype(F32) + term).astype(BF16)
    store_last = pltpu.make_async_copy(backg_ref, backg_hbm, local_sems.at[5])
    store_last.start()

    gather.drain()
    hand_on.wait_send()
    wait_bytes(back_halo, sems.at[16])
    for part in range(3):
        for base in (10, 13):
            wait_bytes(recv.at[pl.ds(0, 31 * PIECE), columns[part]], sems.at[base + part])

    @pl.when(at.y == at.g)
    def _():
        wait_bytes(halo_grad.at[pl.ds(0, 448), :], sems.at[0])

    store.wait()
    store_last.wait()


def per_device(
    upper_out, lower_out, upper_grad, lower_grad, norm_gain, query_weight, key_weight,
    value_matrix, out_weight, route_table, doc_lengths,
):
    rows, width = lower_out.shape
    docs = doc_lengths.shape[1]
    vmem = pl.BlockSpec(memory_space=pltpu.VMEM)
    smem = pl.BlockSpec(memory_space=pltpu.SMEM)
    anywhere = pl.BlockSpec(memory_space=pl.ANY)
    dma = pltpu.SemaphoreType.DMA
    row_block = pltpu.VMEM((rows, width), BF16)
    return pl.pallas_call(
        kernel,
        out_shape=(jax.ShapeDtypeStruct((rows, width), BF16),) * 2,
        in_specs=[anywhere] * 4 + [vmem] * 5 + [smem] * 2,
        out_specs=(anywhere, anywhere),
        scratch_shapes=[row_block] * 6 + [
            pltpu.VMEM((HEADS_KV, RING, RING, 32, GROUP_COLS), BF16),
            row_block,
            pltpu.VMEM((HEADS_KV, rows, GROUP_COLS), BF16),
            pltpu.VMEM((BLOCK, GROUP_COLS), BF16),
            pltpu.VMEM((2 * BLOCK, PAIR), BF16),
            pltpu.VMEM((2 * BLOCK, PAIR), F32),
            pltpu.VMEM((BLOCK, GROUP_COLS), BF16),
            pltpu.VMEM((BLOCK, PAIR), BF16),
            pltpu.VMEM((BLOCK, PAIR), BF16),
            pltpu.VMEM((HEADS_KV, rows, GROUP_COLS), BF16),
            pltpu.VMEM((docs, TILE), jnp.int32),
            pltpu.VMEM((docs, TILE), jnp.int32),
            dma((2, 2, 4)), dma((2, 2, RING, 4)), dma((2, 14)), dma((8,)), dma((18,)), dma((6,)),
        ],
        compiler_params=pltpu.CompilerParams(
            collective_id=0, has_side_effects=True, vmem_limit_bytes=56 * 1024 * 1024
        ),
        name="coupling",
    )(
        lower_out, upper_grad, upper_out, lower_grad, norm_gain.reshape(1, width), query_weight,
        key_weight, value_matrix, out_weight, route_table, doc_lengths,
    )


def solution(mesh):
    rows = P(("grp", "sp"), None)
    return jax.shard_map(
        per_device,
        mesh=mesh,
        in_specs=(
            rows, rows, rows, rows, P(), P("sp", None), P("sp", None), P("sp", None),
            P("sp", None), P("grp", "sp", None), P("grp", None),
        ),
        out_specs=(rows, rows),
        check_vma=False,
    )
```

```python
import functools

import jax
import jax.numpy as jnp
from jax import lax
from jax.experimental import pallas as pl
from jax.experimental.pallas import tpu as pltpu
from jax.sharding import PartitionSpec as P

HEAD = 64
PAIR = 2 * HEAD
PIECE = 16
BLOCK = 512
TILE = 128
WINDOW = BLOCK + TILE
RING = 8
HEADS_KV = 4
GROUP_COLS = 4 * PAIR + PAIR
MESH = pl.DeviceIdType.MESH
F32 = jnp.float32
BF16 = jnp.bfloat16


def dot(a, b):
    return jnp.dot(a, b, preferred_element_type=F32)


def dot_nt(a, b):
    return lax.dot_general(a, b, (((1,), (1,)), ((), ())), preferred_element_type=F32)


def dot_tn(a, b):
    return lax.dot_general(a, b, (((0,), (0,)), ((), ())), preferred_element_type=F32)


def div(a, n):
    return lax.div(a, jnp.int32(n))


def mod(a, n):
    return lax.rem(a, jnp.int32(n))


class Place:
    def __init__(self):
        self.g = lax.axis_index("grp")
        self.s = lax.axis_index("sp")
        self.x, self.core = div(self.g, 2), mod(self.g, 2)
        self.z, self.y = div(self.s, RING), mod(self.s, RING)
        self.zp, self.zb = div(self.z, 2), mod(self.z, 2)
        self.block = self.x * 4 + self.zp
        self.a = self.y
        self.c = self.core + 2 * self.zb
        self.mine = self.c * 8 + self.a
        self.source = self.zb * 16 + self.y * 2 + self.core

    def attender(self, block, c, a):
        return {
            "grp": div(block, 4) * 2 + mod(c, 2),
            "sp": (mod(block, 4) * 2 + div(c, 2)) * RING + a,
        }

    def home(self, block, source):
        return {
            "grp": div(block, 4) * 2 + mod(source, 2),
            "sp": (mod(block, 4) * 2 + div(source, 16)) * RING + mod(div(source, 2), RING),
        }

    def after(self):
        return mod(self.block + 1, 16)

    def before(self):
        return mod(self.block + 15, 16)


def greet(at):
    barrier = pltpu.get_barrier_semaphore()

    def signal(device):
        pl.semaphore_signal(barrier, inc=1, device_id=device, device_id_type=MESH)

    for dz in (1, 2, RING - 2, RING - 1):
        signal({"grp": at.g, "sp": mod(at.z + dz, RING) * RING + at.y})
    signal(at.attender(at.after(), at.c, at.a))
    signal(at.attender(at.before(), at.c, at.a))

    def column(d, carry):
        signal({"grp": mod(at.g + d, 8), "sp": at.s})
        return carry

    def own(d, carry):
        other = mod(at.mine + d, 32)
        signal(at.attender(at.block, div(other, 8), mod(other, 8)))
        return carry

    lax.fori_loop(1, 8, column, 0)
    lax.fori_loop(1, 32, own, 0)
    pl.semaphore_wait(barrier, 4 + 2 + 7 + 31)


def wait_bytes(ref, sem):
    pltpu.make_async_copy(ref, ref, sem).wait()


class Gather:
    def __init__(self, at, full, rest, sems):
        self.at, self.full, self.rest = at, full, rest
        self.first_in, self.second_in, self.share_in, self.cross_in, self.cross_share_in, self.out = sems
        along_y = [mod(at.y + k, RING) for k in range(RING)]
        along_z = [mod(at.z + k, RING) for k in range(RING)]
        self.places = ((along_y, along_z), (along_z, along_y))
        self.crossing = []

    def shard(self, order, core, i1, i2, half):
        z, y = (i2, i1) if order == 0 else (i1, i2)
        units = slice(None) if half is None else (pl.ds(0, 4), pl.ds(4, 3))[half]
        return self.full.at[2 * core + order, z, y, units]

    def line(self, order, core, d):
        j = 2 * core + order
        i2 = self.places[order][1][d]
        return self.full.at[j, i2] if order == 0 else self.full.at[j, :, i2]

    def rest_line(self, order, core, d, slots):
        return self.rest.at[2 * core + order, slots, self.places[order][1][d]]

    def step(self, order, axis, way):
        at = self.at
        if (order + axis) % 2 == 0:
            return {"grp": at.g, "sp": at.z * RING + self.places[0][0][way % RING]}
        return {"grp": at.g, "sp": self.places[0][1][way % RING] * RING + at.y}

    def first(self, order, way, t, arriving):
        half = None if t < 4 else (1 - way) // 2
        hops = 1 if t % 2 else 2
        back = t if arriving else t - hops
        i1 = self.places[order][0][(-way * back) % RING]
        block = self.shard(order, self.at.core, i1, self.places[order][1][0], half)
        return pltpu.make_async_remote_copy(
            src_ref=block, dst_ref=block, send_sem=self.out.at[order],
            recv_sem=self.first_in.at[order, (1 - way) // 2, t - 1],
            device_id=self.step(order, 0, way * hops), device_id_type=MESH,
        )

    def second(self, order, way, k, m, i2):
        half = None if m < 4 else (1 - way) // 2
        i1 = self.places[order][0][k % RING]
        block = self.shard(order, self.at.core, i1, i2, half)
        return pltpu.make_async_remote_copy(
            src_ref=block, dst_ref=block, send_sem=self.out.at[2 + order],
            recv_sem=self.second_in.at[order, (1 - way) // 2, (k + RING) % RING, m - 1],
            device_id=self.step(order, 1, way), device_id_type=MESH,
        )

    def share_block(self, order, core, n):
        if n < 7:
            first, second = self.places[order]
            return self.shard(order, core, first[n + 1], second[0], None)
        return self.line(order, core, n - 6)

    def to_sibling(self, block, send_sem, recv_sem):
        at = self.at
        pltpu.make_async_remote_copy(
            src_ref=block, dst_ref=block, send_sem=send_sem, recv_sem=recv_sem,
            device_id={"grp": at.x * 2 + 1 - at.core, "sp": at.s}, device_id_type=MESH,
        ).start()

    def hand_over(self, order, n):
        self.to_sibling(
            self.share_block(order, self.at.core, n),
            self.out.at[4 + (n >= 7) * 2 + order], self.share_in.at[order, n],
        )

    def cross(self, order, d, source, target, way):
        at = self.at
        return pltpu.make_async_remote_copy(
            src_ref=self.rest_line(order, at.core, d, source),
            dst_ref=self.rest_line(order, at.core, d, target),
            send_sem=self.out.at[8 + order], recv_sem=self.cross_in.at[order, d, target - 1],
            device_id={"grp": mod(at.x + way + 4, 4) * 2 + at.core, "sp": at.s},
            device_id_type=MESH,
        )

    def start_cross(self, order, d):
        j = 2 * self.at.core + order
        i2 = self.places[order][1][d]
        if order == 0:
            self.rest[j, 0, i2] = self.full[j, i2, :, 6]
        else:
            self.rest[j, 0, i2] = self.full[j, :, i2, 6]
        self.cross(order, d, 0, 3, 1).start()
        self.cross(order, d, 0, 1, -1).start()
        self.crossing.append((order, d))

    def forward_cross(self, items):
        for order, d in items:
            self.cross(order, d, 0, 3, 1).wait_recv()
            self.cross(order, d, 0, 1, -1).wait_recv()
            if d % 2 == 0:
                self.cross(order, d, 3, 2, 1).start()
            else:
                self.cross(order, d, 1, 2, -1).start()

    def share_cross(self, items):
        for order, d in items:
            self.cross(order, d, 3, 2, 1).wait_recv()
            self.to_sibling(
                self.rest_line(order, self.at.core, d, pl.ds(1, 3)),
                self.out.at[10 + order], self.cross_share_in.at[order, d],
            )

    def run(self, filler):
        for tick in range(7):
            for order in (0, 1):
                for way in (1, -1):
                    for t in {1: (1, 2), 2: (3, 4)}.get(tick, ()):
                        self.first(order, way, t, True).wait_recv()
                        if t < 4:
                            self.hand_over(order, (-way * t) % RING - 1)
                    for t in {0: (1, 2), 1: (3, 4)}.get(tick, ()):
                        self.first(order, way, t, False).start()
                if tick == 2:
                    self.hand_over(order, 3)
                    self.start_cross(order, 0)
            for k in (3, -3, 4, 2, -2, 1, -1, 0):
                m = tick - (abs(k) + 1) // 2 + 1
                if m < 1 or m > 5:
                    continue
                for order in (0, 1):
                    for way in (1, -1):
                        i2 = self.places[order][1][(-way * (m - 1)) % RING]
                        if m > 1:
                            self.second(order, way, k, m - 1, i2).wait_recv()
                        if m < 5:
                            self.second(order, way, k, m, i2).start()
                        if k == 4 and 1 < m < 5:
                            d = (-way * (m - 1)) % RING
                            self.hand_over(order, 6 + d)
                            self.start_cross(order, d)
                    if k == 4 and m == 5:
                        self.hand_over(order, 10)
                        self.start_cross(order, 4)
                next(filler, None)
        for _ in filler:
            pass
        self.forward_cross(self.crossing[:10])
        for order in (0, 1):
            for n in range(14):
                wait_bytes(
                    self.share_block(order, 1 - self.at.core, n), self.share_in.at[order, n]
                )

    def finish_cross(self):
        self.share_cross(self.crossing)
        for order in (0, 1):
            for d in range(RING):
                wait_bytes(
                    self.rest_line(order, 1 - self.at.core, d, pl.ds(1, 3)),
                    self.cross_share_in.at[order, d],
                )

    def drain(self):
        seven = self.full.at[0, 0, pl.ds(0, 7)]
        lines = self.full.at[0, pl.ds(0, 7)]
        rest = self.rest.at[0, pl.ds(0, 3)]
        for order in (0, 1):
            for n, ref in enumerate((seven, lines, seven, lines, rest, rest)):
                wait_bytes(ref, self.out.at[2 * n + order])


def swap_halves(a):
    return pltpu.roll(a, HEAD, 1)


def two_heads(pair, scale):
    low = lax.broadcasted_iota(jnp.int32, (1, PAIR), 1) < HEAD
    first = jnp.where(low, scale, 0.0).astype(BF16)
    second = jnp.where(low, 0.0, scale).astype(BF16)
    return jnp.concatenate([pair * first, pair * second], axis=0)


def stacked(a):
    return jnp.concatenate([a[:, :TILE], a[:, TILE:]], axis=0)


def attend(at, pair, recv, keys_twice, keys_t, probs, outs, back, ends_ref):
    ends = ends_ref[...]

    def tile(t, carry):
        first = pl.multiple_of(t * TILE, TILE)
        window = pl.ds(first, WINDOW)
        queries = two_heads(recv[pl.ds(first, TILE), PAIR * pair : PAIR * (pair + 1)], 0.125)
        scores = dot_nt(keys_twice[window, :], queries)
        position = at.block * BLOCK + first + lax.broadcasted_iota(jnp.int32, (1, TILE), 1)
        began = jnp.max(jnp.where(ends <= position, ends, 0), axis=0, keepdims=True)
        key_position = (at.block - 1) * BLOCK + first + lax.broadcasted_iota(
            jnp.int32, (WINDOW, TILE), 0
        )
        allowed = (key_position >= began) & (key_position <= position)
        halves = []
        for i in range(2):
            cols = slice(TILE * i, TILE * (i + 1))
            s = jnp.where(allowed, scores[:, cols], -jnp.inf)
            raised = jnp.exp(s - jnp.max(s, axis=0, keepdims=True))
            prob = raised * (1.0 / jnp.sum(raised, axis=0, keepdims=True))
            probs[pair, t, :, cols] = prob
            halves.append(prob.astype(BF16))
        out = stacked(dot(keys_t[HEAD:, window], jnp.concatenate(halves, axis=1)))
        out = out.astype(BF16).astype(F32)
        outs[pair, t] = out
        back[pl.ds(first, TILE), 2 * PAIR * pair : 2 * PAIR * pair + PAIR] = out.T.astype(BF16)
        return carry

    lax.fori_loop(0, BLOCK // TILE, tile, 0)


def differentiate(
    pair, recv, values_twice, keys_t, probs, outs, key_total, value_total, back, finish
):
    def tile(t, carry):
        first = pl.multiple_of(t * TILE, TILE)
        window = pl.ds(first, WINDOW)
        mine = pl.ds(first, TILE)
        queries = two_heads(recv[mine, PAIR * pair : PAIR * (pair + 1)], 0.125)
        grad = recv[mine, 2 * PAIR + PAIR * pair : 2 * PAIR + PAIR * (pair + 1)]
        grads = two_heads(grad, 1.0)
        prob_grad = dot_nt(values_twice[window, :], grads)
        product = grad.astype(F32).T * outs[pair, t]
        halves, slopes = [], []
        for i in range(2):
            cols = slice(TILE * i, TILE * (i + 1))
            delta = jnp.sum(product[HEAD * i : HEAD * (i + 1), :], axis=0, keepdims=True)
            prob = probs[pair, t, :, cols]
            halves.append(prob.astype(BF16))
            slopes.append((prob * (prob_grad[:, cols] - delta)).astype(BF16))
        slope = jnp.concatenate(slopes, axis=1)
        query_grad = stacked(dot(keys_t[:HEAD, window], slope)) * 0.125
        back[mine, 2 * PAIR * pair + PAIR : 2 * PAIR * (pair + 1)] = query_grad.T.astype(BF16)
        key_total[window, :] += dot(slope, queries)
        value_total[window, :] += dot(jnp.concatenate(halves, axis=1), grads)
        finish(first)
        return carry

    lax.fori_loop(0, BLOCK // TILE, tile, 0)


def kernel(
    lower_hbm, ugrad_hbm, uout_hbm, lgrad_hbm, gain_ref, wq_ref, wk_ref, wv_ref, wo_ref,
    route_ref, lens_ref,
    restored_hbm, backg_hbm,
    lower_ref, ugrad_ref, uout_ref, lgrad_ref, restored_ref, backg_ref,
    full, rest, normed, send, recv, keys, keys_twice, values_twice, keys_t, probs, outs,
    key_total, value_total, back, back_halo, halo_grad, ret, ends_own, ends,
    first_in, second_in, share_in, cross_in, cross_share_in, gather_out, sems, local_sems,
):
    at = Place()
    rows, width = lower_ref.shape
    deep = RING * RING * 32
    query_cols = HEADS_KV * 4 * HEAD
    loads = [
        pltpu.make_async_copy(src, dst, local_sems.at[n])
        for n, (src, dst) in enumerate(
            ((lower_hbm, lower_ref), (ugrad_hbm, ugrad_ref), (uout_hbm, uout_ref),
             (lgrad_hbm, lgrad_ref))
        )
    ]
    for load in loads:
        load.start()

    low_w = lax.broadcasted_iota(jnp.int32, (32, PAIR), 1) < HEAD
    for j in range(HEADS_KV):
        k2 = wk_ref[:, PAIR * (j // 2) : PAIR * (j // 2 + 1)].astype(F32)
        v2 = wv_ref[:, PAIR * (j // 2) : PAIR * (j // 2 + 1)].astype(F32)
        if j % 2 == 0:
            kv = jnp.where(low_w, k2, swap_halves(v2))
        else:
            kv = jnp.where(low_w, swap_halves(k2), v2)
        tiles = [wq_ref[:, 256 * j + PAIR * t : 256 * j + PAIR * (t + 1)] for t in range(2)]
        for t, tile in enumerate(tiles + [kv.astype(BF16)]):
            for h in range(2):
                full[j, at.z, at.y, 2 * t + h] = tile[PIECE * h : PIECE * (h + 1), :]
        own = pl.multiple_of(512 * j + PAIR * at.x, PAIR)
        full[j, at.z, at.y, 6] = wo_ref[:, pl.ds(own, PAIR)]
    docs = ends.shape[0]
    doc = lax.broadcasted_iota(jnp.int32, (docs, TILE), 0)
    until = jnp.zeros((docs, TILE), jnp.int32)
    so_far = 0
    for k in range(docs):
        so_far = so_far + lens_ref[0, k]
        until = jnp.where(doc == k, so_far, until)
    ends_own[...] = until
    greet(at)

    @pl.when(at.y == at.g)
    def _():
        def tell(d, carry):
            pltpu.make_async_remote_copy(
                src_ref=ends_own, dst_ref=ends, send_sem=sems.at[0], recv_sem=sems.at[1],
                device_id={"grp": mod(at.g + d, 8), "sp": at.s}, device_id_type=MESH,
            ).start()
            return carry

        lax.fori_loop(1, 8, tell, 0)
        ends[...] = ends_own[...]

    def norm():
        loads[0].wait()
        for r in range(0, rows, PIECE):
            part = lower_ref[r : r + PIECE, :].astype(F32)
            inv = lax.rsqrt(jnp.mean(part * part, axis=1, keepdims=True) + 1e-05)
            normed[r : r + PIECE, :] = ((part * inv) * gain_ref[...]).astype(BF16)
            yield

    gather = Gather(
        at, full, rest, (first_in, second_in, share_in, cross_in, cross_share_in, gather_out)
    )
    gather.run(norm())

    def in_weights(c, tiles=(0, 1, 2)):
        return jnp.concatenate(
            [full[c, :, :, 2 * t : 2 * t + 2].reshape(deep, PAIR) for t in tiles], axis=1
        )

    def out_columns(j, u):
        return pl.ds(pl.multiple_of(512 * j + PAIR * (mod(at.x + u, 4)), PAIR), PAIR)

    def out_weights(j, h):
        parts = []
        for u in (2 * h, 2 * h + 1):
            if u == 0:
                part = full[j, :, :, 6]
            elif j % 2 == 0:
                part = rest[j, u]
            else:
                part = jnp.concatenate([rest[j, u, :, z] for z in range(RING)], axis=0)
            parts.append(part.reshape(query_cols, PAIR))
        return jnp.concatenate(parts, axis=1)

    def piece(i):
        return pl.ds(pl.multiple_of(i * PIECE, PIECE), PIECE)

    columns = (pl.ds(0, 2 * PAIR), pl.ds(2 * PAIR, 2 * PAIR), pl.ds(4 * PAIR, PAIR))

    def put_out(part):
        cols = columns[part]

        def target(source):
            if part == 2:
                return keys.at[pl.ds(pl.multiple_of(BLOCK + source * PIECE, PIECE), PIECE), :]
            return recv.at[piece(source), cols]

        pltpu.make_async_copy(
            send.at[at.c, piece(at.a), cols], target(at.source), sems.at[4 + part]
        ).start()

        def one(d):
            other = mod(at.mine + d, 32)
            c, a = div(other, 8), mod(other, 8)
            pltpu.make_async_remote_copy(
                src_ref=send.at[c, piece(a), cols], dst_ref=target(at.source),
                send_sem=sems.at[10 + part], recv_sem=sems.at[4 + part],
                device_id=at.attender(at.block, c, a), device_id_type=MESH,
            ).start()

        for d in range(1, 32):
            one(d)

    def put_back(part):
        cols = columns[part]
        pltpu.make_async_copy(
            back.at[piece(at.source), cols], ret.at[at.c, piece(at.a), cols], sems.at[7 + part]
        ).start()

        def one(d):
            source = mod(at.source + d, 32)
            pltpu.make_async_remote_copy(
                src_ref=back.at[piece(source), cols], dst_ref=ret.at[at.c, piece(at.a), cols],
                send_sem=sems.at[13 + part], recv_sem=sems.at[7 + part],
                device_id=at.home(at.block, source), device_id_type=MESH,
            ).start()

        for d in range(1, 32):
            one(d)

    row = lax.broadcasted_iota(jnp.int32, (1, rows), 1)
    dest = row % PIECE
    for p in range(rows // PIECE):
        dest = jnp.where(row // PIECE == p, dest + route_ref[0, 0, p] * PIECE, dest)
    permute = (
        lax.broadcasted_iota(jnp.int32, (rows, rows), 0) == dest
    ).astype(F32).astype(BF16)

    for c in range(HEADS_KV):
        if c == 2:
            gather.forward_cross(gather.crossing[10:])
        qkv = dot(normed[...], in_weights(c)).astype(BF16)
        qkv = dot(permute, qkv).astype(BF16)
        send[c, :, : 4 * HEAD] = qkv[:, : 4 * HEAD]
        send[c, :, 8 * HEAD :] = qkv[:, 4 * HEAD :]
    put_out(2)
    put_out(0)
    gather.finish_cross()

    own_keys, old_keys = keys.at[pl.ds(BLOCK, BLOCK), :], keys.at[pl.ds(0, BLOCK), :]
    wait_bytes(own_keys, sems.at[6])
    hand_on = pltpu.make_async_remote_copy(
        src_ref=own_keys, dst_ref=old_keys, send_sem=sems.at[2], recv_sem=sems.at[3],
        device_id=at.attender(at.after(), at.c, at.a), device_id_type=MESH,
    )
    hand_on.start()
    loads[1].wait()
    grad_cols = jnp.zeros((rows, query_cols), F32)
    for j in range(HEADS_KV):
        for h in range(2):
            above = jnp.concatenate(
                [ugrad_ref[:, out_columns(j, u)] for u in (2 * h, 2 * h + 1)], axis=1
            )
            grad_cols = grad_cols + dot_nt(above, out_weights(j, h))
    grad_cols = dot(permute, grad_cols.astype(BF16)).astype(BF16)
    for c in range(HEADS_KV):
        send[c, :, 4 * HEAD : 8 * HEAD] = grad_cols[:, 4 * HEAD * c : 4 * HEAD * (c + 1)]
    put_out(1)
    key_total[...] = jnp.zeros_like(key_total)
    value_total[...] = jnp.zeros_like(value_total)

    @pl.when(at.y != at.g)
    def _():
        wait_bytes(ends, sems.at[1])

    hand_on.wait_recv()
    here = keys[...].astype(F32)
    there = swap_halves(here)
    low_keys = lax.broadcasted_iota(jnp.int32, (2 * BLOCK, PAIR), 1) < HEAD
    keys_twice[...] = jnp.where(low_keys, here, there).astype(BF16)
    values_twice[...] = jnp.where(low_keys, there, here).astype(BF16)
    keys_t[...] = here.T.astype(BF16)

    def key_value_grads(span):
        k, v = key_total[span, :], value_total[span, :]
        low_span = lax.broadcasted_iota(jnp.int32, k.shape, 1) < HEAD
        return jnp.where(low_span, k + swap_halves(k), v + swap_halves(v))

    def hand_back(first):
        done = pl.ds(first, TILE)
        back_halo[done, :] = key_value_grads(done).astype(BF16)
        pltpu.make_async_remote_copy(
            src_ref=back_halo.at[done, :], dst_ref=halo_grad.at[done, :], send_sem=sems.at[16],
            recv_sem=sems.at[17], device_id=at.attender(at.before(), at.c, at.a),
            device_id_type=MESH,
        ).start()

    wait_bytes(recv.at[:, columns[0]], sems.at[4])
    for p in range(2):
        attend(at, p, recv, keys_twice, keys_t, probs, outs, back, ends)
    wait_bytes(recv.at[:, columns[1]], sems.at[5])
    for p in range(2):
        differentiate(
            p, recv, values_twice, keys_t, probs, outs, key_total, value_total, back,
            hand_back if p else lambda first: None,
        )
        put_back(p)
    wait_bytes(halo_grad, sems.at[17])
    back[:, 4 * PAIR :] = (
        key_value_grads(pl.ds(BLOCK, BLOCK)) + halo_grad[...].astype(F32)
    ).astype(BF16)
    put_back(2)

    normed_grad = jnp.zeros((rows, deep), F32)
    attended, slopes = [[] for _ in range(2)], [[] for _ in range(HEADS_KV)]
    for p in range(2):
        wait_bytes(ret.at[:, :, columns[p]], sems.at[7 + p])
        for c in range(HEADS_KV):
            mine = dot_tn(permute, ret[c, :, 2 * PAIR * p : 2 * PAIR * (p + 1)]).astype(BF16)
            attended[p].append(mine[:, :PAIR])
            slopes[c].append(mine[:, PAIR:])
    both = jnp.concatenate([attended[p][c] for c in range(HEADS_KV) for p in range(2)], axis=1)
    loads[2].wait()
    for j in range(HEADS_KV):
        for h in range(2):
            mixed = dot(both, out_weights(j, h))
            for i in range(2):
                cols = out_columns(j, 2 * h + i)
                restored_ref[:, cols] = (
                    uout_ref[:, cols].astype(F32) - mixed[:, PAIR * i : PAIR * (i + 1)]
                ).astype(BF16)
    store = pltpu.make_async_copy(restored_ref, restored_hbm, local_sems.at[4])
    store.start()
    for c in range(HEADS_KV):
        normed_grad = normed_grad + dot_nt(
            jnp.concatenate(slopes[c], axis=1), in_weights(c, (0, 1))
        )
    low_f = lower_ref[...].astype(F32)
    inv = lax.rsqrt(jnp.mean(low_f * low_f, axis=1, keepdims=True) + 1e-05)
    unit = low_f * inv
    loads[3].wait()
    wait_bytes(ret.at[:, :, columns[2]], sems.at[9])
    for c in range(0, HEADS_KV, 2):
        both = jnp.concatenate([ret[c, :, 4 * PAIR :], ret[c + 1, :, 4 * PAIR :]], axis=1)
        both = dot_tn(permute, both).astype(BF16)
        weights = jnp.concatenate([in_weights(c, (2,)), in_weights(c + 1, (2,))], axis=1)
        normed_grad = normed_grad + dot_nt(both, weights)
    unit_grad = normed_grad * gain_ref[...]
    term = inv * (unit_grad - unit * jnp.mean(unit_grad * unit, axis=1, keepdims=True))
    backg_ref[...] = (lgrad_ref[...].astype(F32) + term).astype(BF16)
    store_last = pltpu.make_async_copy(backg_ref, backg_hbm, local_sems.at[5])
    store_last.start()

    gather.drain()
    hand_on.wait_send()
    wait_bytes(back_halo, sems.at[16])
    for part in range(3):
        for base in (10, 13):
            wait_bytes(recv.at[pl.ds(0, 31 * PIECE), columns[part]], sems.at[base + part])

    @pl.when(at.y == at.g)
    def _():
        wait_bytes(halo_grad.at[pl.ds(0, 448), :], sems.at[0])

    store.wait()
    store_last.wait()


def per_device(
    upper_out, lower_out, upper_grad, lower_grad, norm_gain, query_weight, key_weight,
    value_matrix, out_weight, route_table, doc_lengths,
):
    rows, width = lower_out.shape
    docs = doc_lengths.shape[1]
    vmem = pl.BlockSpec(memory_space=pltpu.VMEM)
    smem = pl.BlockSpec(memory_space=pltpu.SMEM)
    anywhere = pl.BlockSpec(memory_space=pl.ANY)
    dma = pltpu.SemaphoreType.DMA
    row_block = pltpu.VMEM((rows, width), BF16)
    return pl.pallas_call(
        kernel,
        out_shape=(jax.ShapeDtypeStruct((rows, width), BF16),) * 2,
        in_specs=[anywhere] * 4 + [vmem] * 5 + [smem] * 2,
        out_specs=(anywhere, anywhere),
        scratch_shapes=[row_block] * 6 + [
            pltpu.VMEM((HEADS_KV, RING, RING, 7, PIECE, PAIR), BF16),
            pltpu.VMEM((HEADS_KV, 4, RING, RING, PIECE, PAIR), BF16),
            row_block,
            pltpu.VMEM((HEADS_KV, rows, GROUP_COLS), BF16),
            pltpu.VMEM((BLOCK, GROUP_COLS), BF16),
            pltpu.VMEM((2 * BLOCK, PAIR), BF16),
            pltpu.VMEM((2 * BLOCK, PAIR), BF16),
            pltpu.VMEM((2 * BLOCK, PAIR), BF16),
            pltpu.VMEM((PAIR, 2 * BLOCK), BF16),
            pltpu.VMEM((2, BLOCK // TILE, WINDOW, 2 * TILE), F32),
            pltpu.VMEM((2, BLOCK // TILE, PAIR, TILE), F32),
            pltpu.VMEM((2 * BLOCK, PAIR), F32),
            pltpu.VMEM((2 * BLOCK, PAIR), F32),
            pltpu.VMEM((BLOCK, GROUP_COLS), BF16),
            pltpu.VMEM((BLOCK, PAIR), BF16),
            pltpu.VMEM((BLOCK, PAIR), BF16),
            pltpu.VMEM((HEADS_KV, rows, GROUP_COLS), BF16),
            pltpu.VMEM((docs, TILE), jnp.int32),
            pltpu.VMEM((docs, TILE), jnp.int32),
            dma((2, 2, 4)), dma((2, 2, RING, 4)), dma((2, 14)), dma((2, RING, 3)), dma((2, RING)),
            dma((12,)), dma((18,)), dma((6,)),
        ],
        compiler_params=pltpu.CompilerParams(
            collective_id=0, has_side_effects=True, vmem_limit_bytes=56 * 1024 * 1024
        ),
        name="coupling",
    )(
        lower_out, upper_grad, upper_out, lower_grad, norm_gain.reshape(1, width), query_weight,
        key_weight, value_matrix, out_weight, route_table, doc_lengths,
    )


def solution(mesh):
    rows = P(("grp", "sp"), None)
    return jax.shard_map(
        per_device,
        mesh=mesh,
        in_specs=(
            rows, rows, rows, rows, P(), P("sp", None), P("sp", None), P("sp", None),
            P("sp", None), P("grp", "sp", None), P("grp", None),
        ),
        out_specs=(rows, rows),
        check_vma=False,
    )
```

```python
import functools

import jax
import jax.numpy as jnp
from jax import lax
from jax.experimental import pallas as pl
from jax.experimental.pallas import tpu as pltpu
from jax.sharding import PartitionSpec as P

HEAD = 64
PAIR = 2 * HEAD
PIECE = 16
BLOCK = 512
TILE = 128
WINDOW = BLOCK + TILE
RING = 8
HEADS_KV = 4
GROUP_COLS = 4 * PAIR + PAIR
MESH = pl.DeviceIdType.MESH
F32 = jnp.float32
BF16 = jnp.bfloat16


def dot(a, b):
    return jnp.dot(a, b, preferred_element_type=F32)


def dot_nt(a, b):
    return lax.dot_general(a, b, (((1,), (1,)), ((), ())), preferred_element_type=F32)


def dot_tn(a, b):
    return lax.dot_general(a, b, (((0,), (0,)), ((), ())), preferred_element_type=F32)


def div(a, n):
    return lax.div(a, jnp.int32(n))


def mod(a, n):
    return lax.rem(a, jnp.int32(n))


class Place:
    def __init__(self):
        self.g = lax.axis_index("grp")
        self.s = lax.axis_index("sp")
        self.x, self.core = div(self.g, 2), mod(self.g, 2)
        self.z, self.y = div(self.s, RING), mod(self.s, RING)
        self.zp, self.zb = div(self.z, 2), mod(self.z, 2)
        self.block = self.x * 4 + self.zp
        self.a = self.y
        self.c = self.core + 2 * self.zb
        self.mine = self.c * 8 + self.a
        self.source = self.zb * 16 + self.y * 2 + self.core

    def attender(self, block, c, a):
        return {
            "grp": div(block, 4) * 2 + mod(c, 2),
            "sp": (mod(block, 4) * 2 + div(c, 2)) * RING + a,
        }

    def home(self, block, source):
        return {
            "grp": div(block, 4) * 2 + mod(source, 2),
            "sp": (mod(block, 4) * 2 + div(source, 16)) * RING + mod(div(source, 2), RING),
        }

    def after(self):
        return mod(self.block + 1, 16)

    def before(self):
        return mod(self.block + 15, 16)


def greet(at):
    barrier = pltpu.get_barrier_semaphore()

    def signal(device):
        pl.semaphore_signal(barrier, inc=1, device_id=device, device_id_type=MESH)

    for dz in (1, 2, RING - 2, RING - 1):
        signal({"grp": at.g, "sp": mod(at.z + dz, RING) * RING + at.y})
    signal(at.attender(at.after(), at.c, at.a))
    signal(at.attender(at.before(), at.c, at.a))

    def column(d, carry):
        signal({"grp": mod(at.g + d, 8), "sp": at.s})
        return carry

    def own(d, carry):
        other = mod(at.mine + d, 32)
        signal(at.attender(at.block, div(other, 8), mod(other, 8)))
        return carry

    lax.fori_loop(1, 8, column, 0)
    lax.fori_loop(1, 32, own, 0)
    return lambda: pl.semaphore_wait(barrier, 4 + 2 + 7 + 31)


def wait_bytes(ref, sem):
    pltpu.make_async_copy(ref, ref, sem).wait()


class Gather:
    def __init__(self, at, full, rest, sems):
        self.at, self.full, self.rest = at, full, rest
        self.first_in, self.second_in, self.share_in, self.cross_in, self.cross_share_in, self.out = sems
        along_y = [mod(at.y + k, RING) for k in range(RING)]
        along_z = [mod(at.z + k, RING) for k in range(RING)]
        self.places = ((along_y, along_z), (along_z, along_y))
        self.crossing = []

    def shard(self, order, core, i1, i2, half):
        z, y = (i2, i1) if order == 0 else (i1, i2)
        units = slice(None) if half is None else (pl.ds(0, 4), pl.ds(4, 3))[half]
        return self.full.at[2 * core + order, z, y, units]

    def line(self, order, core, d):
        j = 2 * core + order
        i2 = self.places[order][1][d]
        return self.full.at[j, i2] if order == 0 else self.full.at[j, :, i2]

    def rest_line(self, order, core, d, slots):
        return self.rest.at[2 * core + order, slots, self.places[order][1][d]]

    def step(self, order, axis, way):
        at = self.at
        if (order + axis) % 2 == 0:
            return {"grp": at.g, "sp": at.z * RING + self.places[0][0][way % RING]}
        return {"grp": at.g, "sp": self.places[0][1][way % RING] * RING + at.y}

    def first(self, order, way, t, arriving):
        half = None if t < 4 else (1 - way) // 2
        hops = 1 if t % 2 else 2
        back = t if arriving else t - hops
        i1 = self.places[order][0][(-way * back) % RING]
        block = self.shard(order, self.at.core, i1, self.places[order][1][0], half)
        return pltpu.make_async_remote_copy(
            src_ref=block, dst_ref=block, send_sem=self.out.at[order],
            recv_sem=self.first_in.at[order, (1 - way) // 2, t - 1],
            device_id=self.step(order, 0, way * hops), device_id_type=MESH,
        )

    def second(self, order, way, k, m, i2):
        half = None if m < 4 else (1 - way) // 2
        i1 = self.places[order][0][k % RING]
        block = self.shard(order, self.at.core, i1, i2, half)
        return pltpu.make_async_remote_copy(
            src_ref=block, dst_ref=block, send_sem=self.out.at[2 + order],
            recv_sem=self.second_in.at[order, (1 - way) // 2, (k + RING) % RING, m - 1],
            device_id=self.step(order, 1, way), device_id_type=MESH,
        )

    def share_block(self, order, core, n):
        if n < 7:
            first, second = self.places[order]
            return self.shard(order, core, first[n + 1], second[0], None)
        return self.line(order, core, n - 6)

    def to_sibling(self, block, send_sem, recv_sem):
        at = self.at
        pltpu.make_async_remote_copy(
            src_ref=block, dst_ref=block, send_sem=send_sem, recv_sem=recv_sem,
            device_id={"grp": at.x * 2 + 1 - at.core, "sp": at.s}, device_id_type=MESH,
        ).start()

    def hand_over(self, order, n):
        self.to_sibling(
            self.share_block(order, self.at.core, n),
            self.out.at[4 + (n >= 7) * 2 + order], self.share_in.at[order, n],
        )

    def cross(self, order, d, source, target, way):
        at = self.at
        return pltpu.make_async_remote_copy(
            src_ref=self.rest_line(order, at.core, d, source),
            dst_ref=self.rest_line(order, at.core, d, target),
            send_sem=self.out.at[8 + order], recv_sem=self.cross_in.at[order, d, target - 1],
            device_id={"grp": mod(at.x + way + 4, 4) * 2 + at.core, "sp": at.s},
            device_id_type=MESH,
        )

    def start_cross(self, order, d):
        j = 2 * self.at.core + order
        i2 = self.places[order][1][d]
        if order == 0:
            self.rest[j, 0, i2] = self.full[j, i2, :, 6]
        else:
            self.rest[j, 0, i2] = self.full[j, :, i2, 6]
        self.cross(order, d, 0, 3, 1).start()
        self.cross(order, d, 0, 1, -1).start()
        self.crossing.append((order, d))

    def forward_cross(self, items):
        for order, d in items:
            self.cross(order, d, 0, 3, 1).wait_recv()
            self.cross(order, d, 0, 1, -1).wait_recv()
            if d % 2 == 0:
                self.cross(order, d, 3, 2, 1).start()
            else:
                self.cross(order, d, 1, 2, -1).start()

    def share_cross(self, items):
        for order, d in items:
            self.cross(order, d, 3, 2, 1).wait_recv()
            self.to_sibling(
                self.rest_line(order, self.at.core, d, pl.ds(1, 3)),
                self.out.at[10 + order], self.cross_share_in.at[order, d],
            )

    def run(self, filler):
        for tick in range(7):
            for order in (0, 1):
                for way in (1, -1):
                    for t in {1: (1, 2), 2: (3, 4)}.get(tick, ()):
                        self.first(order, way, t, True).wait_recv()
                        if t < 4:
                            self.hand_over(order, (-way * t) % RING - 1)
                    for t in {0: (1, 2), 1: (3, 4)}.get(tick, ()):
                        self.first(order, way, t, False).start()
                if tick == 2:
                    self.hand_over(order, 3)
                    self.start_cross(order, 0)
            for k in (3, -3, 4, 2, -2, 1, -1, 0):
                m = tick - (abs(k) + 1) // 2 + 1
                if m < 1 or m > 5:
                    continue
                for order in (0, 1):
                    for way in (1, -1):
                        i2 = self.places[order][1][(-way * (m - 1)) % RING]
                        if m > 1:
                            self.second(order, way, k, m - 1, i2).wait_recv()
                        if m < 5:
                            self.second(order, way, k, m, i2).start()
                        if k == 4 and 1 < m < 5:
                            d = (-way * (m - 1)) % RING
                            self.hand_over(order, 6 + d)
                            self.start_cross(order, d)
                    if k == 4 and m == 5:
                        self.hand_over(order, 10)
                        self.start_cross(order, 4)
                next(filler, None)
        for _ in filler:
            pass
        self.forward_cross(self.crossing[:10])
        for order in (0, 1):
            for n in range(14):
                wait_bytes(
                    self.share_block(order, 1 - self.at.core, n), self.share_in.at[order, n]
                )

    def finish_cross(self):
        self.share_cross(self.crossing)
        for order in (0, 1):
            for d in range(RING):
                wait_bytes(
                    self.rest_line(order, 1 - self.at.core, d, pl.ds(1, 3)),
                    self.cross_share_in.at[order, d],
                )

    def drain(self):
        seven = self.full.at[0, 0, pl.ds(0, 7)]
        lines = self.full.at[0, pl.ds(0, 7)]
        rest = self.rest.at[0, pl.ds(0, 3)]
        for order in (0, 1):
            for n, ref in enumerate((seven, lines, seven, lines, rest, rest)):
                wait_bytes(ref, self.out.at[2 * n + order])


def swap_halves(a):
    return pltpu.roll(a, HEAD, 1)


def two_heads(pair, scale):
    low = lax.broadcasted_iota(jnp.int32, (1, PAIR), 1) < HEAD
    first = jnp.where(low, scale, 0.0).astype(BF16)
    second = jnp.where(low, 0.0, scale).astype(BF16)
    return jnp.concatenate([pair * first, pair * second], axis=0)


def stacked(a):
    return jnp.concatenate([a[:, :TILE], a[:, TILE:]], axis=0)


def attend(at, pair, recv, keys_twice, keys_t, probs, outs, back, ends_ref):
    ends = ends_ref[...]

    def tile(t, carry):
        first = pl.multiple_of(t * TILE, TILE)
        window = pl.ds(first, WINDOW)
        queries = two_heads(recv[pl.ds(first, TILE), PAIR * pair : PAIR * (pair + 1)], 0.125)
        scores = dot_nt(keys_twice[window, :], queries)
        position = at.block * BLOCK + first + lax.broadcasted_iota(jnp.int32, (1, TILE), 1)
        began = jnp.max(jnp.where(ends <= position, ends, 0), axis=0, keepdims=True)
        key_position = (at.block - 1) * BLOCK + first + lax.broadcasted_iota(
            jnp.int32, (WINDOW, TILE), 0
        )
        allowed = (key_position >= began) & (key_position <= position)
        halves = []
        for i in range(2):
            cols = slice(TILE * i, TILE * (i + 1))
            s = jnp.where(allowed, scores[:, cols], -jnp.inf)
            raised = jnp.exp(s - jnp.max(s, axis=0, keepdims=True))
            prob = raised * (1.0 / jnp.sum(raised, axis=0, keepdims=True))
            probs[pair, t, :, cols] = prob
            halves.append(prob.astype(BF16))
        out = stacked(dot(keys_t[HEAD:, window], jnp.concatenate(halves, axis=1)))
        out = out.astype(BF16).astype(F32)
        outs[pair, t] = out
        back[pl.ds(first, TILE), 2 * PAIR * pair : 2 * PAIR * pair + PAIR] = out.T.astype(BF16)
        return carry

    lax.fori_loop(0, BLOCK // TILE, tile, 0)


def differentiate(
    pair, recv, values_twice, keys_t, probs, outs, key_total, value_total, back, finish
):
    def tile(t, carry):
        first = pl.multiple_of(t * TILE, TILE)
        window = pl.ds(first, WINDOW)
        mine = pl.ds(first, TILE)
        queries = two_heads(recv[mine, PAIR * pair : PAIR * (pair + 1)], 0.125)
        grad = recv[mine, 2 * PAIR + PAIR * pair : 2 * PAIR + PAIR * (pair + 1)]
        grads = two_heads(grad, 1.0)
        prob_grad = dot_nt(values_twice[window, :], grads)
        product = grad.astype(F32).T * outs[pair, t]
        halves, slopes = [], []
        for i in range(2):
            cols = slice(TILE * i, TILE * (i + 1))
            delta = jnp.sum(product[HEAD * i : HEAD * (i + 1), :], axis=0, keepdims=True)
            prob = probs[pair, t, :, cols]
            halves.append(prob.astype(BF16))
            slopes.append((prob * (prob_grad[:, cols] - delta)).astype(BF16))
        slope = jnp.concatenate(slopes, axis=1)
        query_grad = stacked(dot(keys_t[:HEAD, window], slope)) * 0.125
        back[mine, 2 * PAIR * pair + PAIR : 2 * PAIR * (pair + 1)] = query_grad.T.astype(BF16)
        key_total[window, :] += dot(slope, queries)
        value_total[window, :] += dot(jnp.concatenate(halves, axis=1), grads)
        finish(first)
        return carry

    lax.fori_loop(0, BLOCK // TILE, tile, 0)


def kernel(
    lower_hbm, ugrad_hbm, uout_hbm, lgrad_hbm, gain_ref, wq_ref, wk_ref, wv_ref, wo_ref,
    route_ref, lens_ref,
    restored_hbm, backg_hbm,
    lower_ref, ugrad_ref, uout_ref, lgrad_ref, restored_ref, backg_ref,
    full, rest, normed, send, recv, keys, keys_twice, values_twice, keys_t, probs, outs,
    key_total, value_total, back, back_halo, halo_grad, ret, ends_own, ends,
    first_in, second_in, share_in, cross_in, cross_share_in, gather_out, sems, local_sems,
):
    at = Place()
    rows, width = lower_ref.shape
    deep = RING * RING * 32
    query_cols = HEADS_KV * 4 * HEAD
    loads = [
        pltpu.make_async_copy(src, dst, local_sems.at[n])
        for n, (src, dst) in enumerate(
            ((lower_hbm, lower_ref), (ugrad_hbm, ugrad_ref), (uout_hbm, uout_ref),
             (lgrad_hbm, lgrad_ref))
        )
    ]
    for load in loads:
        load.start()
    greeted = greet(at)

    low_w = lax.broadcasted_iota(jnp.int32, (32, PAIR), 1) < HEAD
    for j in range(HEADS_KV):
        k2 = wk_ref[:, PAIR * (j // 2) : PAIR * (j // 2 + 1)].astype(F32)
        v2 = wv_ref[:, PAIR * (j // 2) : PAIR * (j // 2 + 1)].astype(F32)
        if j % 2 == 0:
            kv = jnp.where(low_w, k2, swap_halves(v2))
        else:
            kv = jnp.where(low_w, swap_halves(k2), v2)
        tiles = [wq_ref[:, 256 * j + PAIR * t : 256 * j + PAIR * (t + 1)] for t in range(2)]
        for t, tile in enumerate(tiles + [kv.astype(BF16)]):
            for h in range(2):
                full[j, at.z, at.y, 2 * t + h] = tile[PIECE * h : PIECE * (h + 1), :]
        own = pl.multiple_of(512 * j + PAIR * at.x, PAIR)
        full[j, at.z, at.y, 6] = wo_ref[:, pl.ds(own, PAIR)]
    docs = ends.shape[0]
    doc = lax.broadcasted_iota(jnp.int32, (docs, TILE), 0)
    until = jnp.zeros((docs, TILE), jnp.int32)
    so_far = 0
    for k in range(docs):
        so_far = so_far + lens_ref[0, k]
        until = jnp.where(doc == k, so_far, until)
    ends_own[...] = until
    greeted()

    @pl.when(at.y == at.g)
    def _():
        def tell(d, carry):
            pltpu.make_async_remote_copy(
                src_ref=ends_own, dst_ref=ends, send_sem=sems.at[0], recv_sem=sems.at[1],
                device_id={"grp": mod(at.g + d, 8), "sp": at.s}, device_id_type=MESH,
            ).start()
            return carry

        lax.fori_loop(1, 8, tell, 0)
        ends[...] = ends_own[...]

    def norm():
        loads[0].wait()
        for r in range(0, rows, PIECE):
            part = lower_ref[r : r + PIECE, :].astype(F32)
            inv = lax.rsqrt(jnp.mean(part * part, axis=1, keepdims=True) + 1e-05)
            normed[r : r + PIECE, :] = ((part * inv) * gain_ref[...]).astype(BF16)
            yield

    gather = Gather(
        at, full, rest, (first_in, second_in, share_in, cross_in, cross_share_in, gather_out)
    )
    gather.run(norm())

    def in_weights(c, tiles=(0, 1, 2)):
        return jnp.concatenate(
            [full[c, :, :, 2 * t : 2 * t + 2].reshape(deep, PAIR) for t in tiles], axis=1
        )

    def out_columns(j, u):
        return pl.ds(pl.multiple_of(512 * j + PAIR * (mod(at.x + u, 4)), PAIR), PAIR)

    def out_weights(j, h):
        parts = []
        for u in (2 * h, 2 * h + 1):
            if u == 0:
                part = full[j, :, :, 6]
            elif j % 2 == 0:
                part = rest[j, u]
            else:
                part = jnp.concatenate([rest[j, u, :, z] for z in range(RING)], axis=0)
            parts.append(part.reshape(query_cols, PAIR))
        return jnp.concatenate(parts, axis=1)

    def piece(i):
        return pl.ds(pl.multiple_of(i * PIECE, PIECE), PIECE)

    columns = (pl.ds(0, 2 * PAIR), pl.ds(2 * PAIR, 2 * PAIR), pl.ds(4 * PAIR, PAIR))

    def put_out(part):
        cols = columns[part]

        def target(source):
            if part == 2:
                return keys.at[pl.ds(pl.multiple_of(BLOCK + source * PIECE, PIECE), PIECE), :]
            return recv.at[piece(source), cols]

        pltpu.make_async_copy(
            send.at[at.c, piece(at.a), cols], target(at.source), sems.at[4 + part]
        ).start()

        def one(d):
            other = mod(at.mine + d, 32)
            c, a = div(other, 8), mod(other, 8)
            pltpu.make_async_remote_copy(
                src_ref=send.at[c, piece(a), cols], dst_ref=target(at.source),
                send_sem=sems.at[10 + part], recv_sem=sems.at[4 + part],
                device_id=at.attender(at.block, c, a), device_id_type=MESH,
            ).start()

        for d in range(1, 32):
            one(d)

    def put_back(part):
        cols = columns[part]
        pltpu.make_async_copy(
            back.at[piece(at.source), cols], ret.at[at.c, piece(at.a), cols], sems.at[7 + part]
        ).start()

        def one(d):
            source = mod(at.source + d, 32)
            pltpu.make_async_remote_copy(
                src_ref=back.at[piece(source), cols], dst_ref=ret.at[at.c, piece(at.a), cols],
                send_sem=sems.at[13 + part], recv_sem=sems.at[7 + part],
                device_id=at.home(at.block, source), device_id_type=MESH,
            ).start()

        for d in range(1, 32):
            one(d)

    row = lax.broadcasted_iota(jnp.int32, (1, rows), 1)
    dest = row % PIECE
    for p in range(rows // PIECE):
        dest = jnp.where(row // PIECE == p, dest + route_ref[0, 0, p] * PIECE, dest)
    permute = (
        lax.broadcasted_iota(jnp.int32, (rows, rows), 0) == dest
    ).astype(F32).astype(BF16)

    for c in range(HEADS_KV):
        if c == 2:
            gather.forward_cross(gather.crossing[10:])
        qkv = dot(normed[...], in_weights(c)).astype(BF16)
        qkv = dot(permute, qkv).astype(BF16)
        send[c, :, : 4 * HEAD] = qkv[:, : 4 * HEAD]
        send[c, :, 8 * HEAD :] = qkv[:, 4 * HEAD :]
    put_out(2)
    put_out(0)
    gather.finish_cross()

    own_keys, old_keys = keys.at[pl.ds(BLOCK, BLOCK), :], keys.at[pl.ds(0, BLOCK), :]
    wait_bytes(own_keys, sems.at[6])
    hand_on = pltpu.make_async_remote_copy(
        src_ref=own_keys, dst_ref=old_keys, send_sem=sems.at[2], recv_sem=sems.at[3],
        device_id=at.attender(at.after(), at.c, at.a), device_id_type=MESH,
    )
    hand_on.start()
    loads[1].wait()
    grad_cols = jnp.zeros((rows, query_cols), F32)
    for j in range(HEADS_KV):
        for h in range(2):
            above = jnp.concatenate(
                [ugrad_ref[:, out_columns(j, u)] for u in (2 * h, 2 * h + 1)], axis=1
            )
            grad_cols = grad_cols + dot_nt(above, out_weights(j, h))
    grad_cols = dot(permute, grad_cols.astype(BF16)).astype(BF16)
    for c in range(HEADS_KV):
        send[c, :, 4 * HEAD : 8 * HEAD] = grad_cols[:, 4 * HEAD * c : 4 * HEAD * (c + 1)]
    put_out(1)
    key_total[...] = jnp.zeros_like(key_total)
    value_total[...] = jnp.zeros_like(value_total)

    @pl.when(at.y != at.g)
    def _():
        wait_bytes(ends, sems.at[1])

    hand_on.wait_recv()
    here = keys[...].astype(F32)
    there = swap_halves(here)
    low_keys = lax.broadcasted_iota(jnp.int32, (2 * BLOCK, PAIR), 1) < HEAD
    keys_twice[...] = jnp.where(low_keys, here, there).astype(BF16)
    values_twice[...] = jnp.where(low_keys, there, here).astype(BF16)
    keys_t[...] = here.T.astype(BF16)

    def key_value_grads(span):
        k, v = key_total[span, :], value_total[span, :]
        low_span = lax.broadcasted_iota(jnp.int32, k.shape, 1) < HEAD
        return jnp.where(low_span, k + swap_halves(k), v + swap_halves(v))

    def hand_back(first):
        done = pl.ds(first, TILE)
        back_halo[done, :] = key_value_grads(done).astype(BF16)
        pltpu.make_async_remote_copy(
            src_ref=back_halo.at[done, :], dst_ref=halo_grad.at[done, :], send_sem=sems.at[16],
            recv_sem=sems.at[17], device_id=at.attender(at.before(), at.c, at.a),
            device_id_type=MESH,
        ).start()

    wait_bytes(recv.at[:, columns[0]], sems.at[4])
    for p in range(2):
        attend(at, p, recv, keys_twice, keys_t, probs, outs, back, ends)
    wait_bytes(recv.at[:, columns[1]], sems.at[5])
    for p in range(2):
        differentiate(
            p, recv, values_twice, keys_t, probs, outs, key_total, value_total, back,
            hand_back if p else lambda first: None,
        )
        put_back(p)
    wait_bytes(halo_grad, sems.at[17])
    back[:, 4 * PAIR :] = (
        key_value_grads(pl.ds(BLOCK, BLOCK)) + halo_grad[...].astype(F32)
    ).astype(BF16)
    put_back(2)

    normed_grad = jnp.zeros((rows, deep), F32)
    attended, slopes = [[] for _ in range(2)], [[] for _ in range(HEADS_KV)]
    for p in range(2):
        wait_bytes(ret.at[:, :, columns[p]], sems.at[7 + p])
        for c in range(HEADS_KV):
            mine = dot_tn(permute, ret[c, :, 2 * PAIR * p : 2 * PAIR * (p + 1)]).astype(BF16)
            attended[p].append(mine[:, :PAIR])
            slopes[c].append(mine[:, PAIR:])
    both = jnp.concatenate([attended[p][c] for c in range(HEADS_KV) for p in range(2)], axis=1)
    loads[2].wait()
    for j in range(HEADS_KV):
        for h in range(2):
            mixed = dot(both, out_weights(j, h))
            for i in range(2):
                cols = out_columns(j, 2 * h + i)
                restored_ref[:, cols] = (
                    uout_ref[:, cols].astype(F32) - mixed[:, PAIR * i : PAIR * (i + 1)]
                ).astype(BF16)
    store = pltpu.make_async_copy(restored_ref, restored_hbm, local_sems.at[4])
    store.start()
    for c in range(HEADS_KV):
        normed_grad = normed_grad + dot_nt(
            jnp.concatenate(slopes[c], axis=1), in_weights(c, (0, 1))
        )
    low_f = lower_ref[...].astype(F32)
    inv = lax.rsqrt(jnp.mean(low_f * low_f, axis=1, keepdims=True) + 1e-05)
    unit = low_f * inv
    loads[3].wait()
    wait_bytes(ret.at[:, :, columns[2]], sems.at[9])
    for c in range(0, HEADS_KV, 2):
        both = jnp.concatenate([ret[c, :, 4 * PAIR :], ret[c + 1, :, 4 * PAIR :]], axis=1)
        both = dot_tn(permute, both).astype(BF16)
        weights = jnp.concatenate([in_weights(c, (2,)), in_weights(c + 1, (2,))], axis=1)
        normed_grad = normed_grad + dot_nt(both, weights)
    unit_grad = normed_grad * gain_ref[...]
    term = inv * (unit_grad - unit * jnp.mean(unit_grad * unit, axis=1, keepdims=True))
    backg_ref[...] = (lgrad_ref[...].astype(F32) + term).astype(BF16)
    store_last = pltpu.make_async_copy(backg_ref, backg_hbm, local_sems.at[5])
    store_last.start()

    gather.drain()
    hand_on.wait_send()
    wait_bytes(back_halo, sems.at[16])
    for part in range(3):
        for base in (10, 13):
            wait_bytes(recv.at[pl.ds(0, 31 * PIECE), columns[part]], sems.at[base + part])

    @pl.when(at.y == at.g)
    def _():
        wait_bytes(halo_grad.at[pl.ds(0, 448), :], sems.at[0])

    store.wait()
    store_last.wait()


def per_device(
    upper_out, lower_out, upper_grad, lower_grad, norm_gain, query_weight, key_weight,
    value_matrix, out_weight, route_table, doc_lengths,
):
    rows, width = lower_out.shape
    docs = doc_lengths.shape[1]
    vmem = pl.BlockSpec(memory_space=pltpu.VMEM)
    smem = pl.BlockSpec(memory_space=pltpu.SMEM)
    anywhere = pl.BlockSpec(memory_space=pl.ANY)
    dma = pltpu.SemaphoreType.DMA
    row_block = pltpu.VMEM((rows, width), BF16)
    return pl.pallas_call(
        kernel,
        out_shape=(jax.ShapeDtypeStruct((rows, width), BF16),) * 2,
        in_specs=[anywhere] * 4 + [vmem] * 5 + [smem] * 2,
        out_specs=(anywhere, anywhere),
        scratch_shapes=[row_block] * 6 + [
            pltpu.VMEM((HEADS_KV, RING, RING, 7, PIECE, PAIR), BF16),
            pltpu.VMEM((HEADS_KV, 4, RING, RING, PIECE, PAIR), BF16),
            row_block,
            pltpu.VMEM((HEADS_KV, rows, GROUP_COLS), BF16),
            pltpu.VMEM((BLOCK, GROUP_COLS), BF16),
            pltpu.VMEM((2 * BLOCK, PAIR), BF16),
            pltpu.VMEM((2 * BLOCK, PAIR), BF16),
            pltpu.VMEM((2 * BLOCK, PAIR), BF16),
            pltpu.VMEM((PAIR, 2 * BLOCK), BF16),
            pltpu.VMEM((2, BLOCK // TILE, WINDOW, 2 * TILE), F32),
            pltpu.VMEM((2, BLOCK // TILE, PAIR, TILE), F32),
            pltpu.VMEM((2 * BLOCK, PAIR), F32),
            pltpu.VMEM((2 * BLOCK, PAIR), F32),
            pltpu.VMEM((BLOCK, GROUP_COLS), BF16),
            pltpu.VMEM((BLOCK, PAIR), BF16),
            pltpu.VMEM((BLOCK, PAIR), BF16),
            pltpu.VMEM((HEADS_KV, rows, GROUP_COLS), BF16),
            pltpu.VMEM((docs, TILE), jnp.int32),
            pltpu.VMEM((docs, TILE), jnp.int32),
            dma((2, 2, 4)), dma((2, 2, RING, 4)), dma((2, 14)), dma((2, RING, 3)), dma((2, RING)),
            dma((12,)), dma((18,)), dma((6,)),
        ],
        compiler_params=pltpu.CompilerParams(
            collective_id=0, has_side_effects=True, vmem_limit_bytes=56 * 1024 * 1024
        ),
        name="coupling",
    )(
        lower_out, upper_grad, upper_out, lower_grad, norm_gain.reshape(1, width), query_weight,
        key_weight, value_matrix, out_weight, route_table, doc_lengths,
    )


def solution(mesh):
    rows = P(("grp", "sp"), None)
    return jax.shard_map(
        per_device,
        mesh=mesh,
        in_specs=(
            rows, rows, rows, rows, P(), P("sp", None), P("sp", None), P("sp", None),
            P("sp", None), P("grp", "sp", None), P("grp", None),
        ),
        out_specs=(rows, rows),
        check_vma=False,
    )
```
